32 devices in a mesh: gx: 4 (over z), gy: 8 (over y, x, core).
Axes of the slice: x: 2, y: 2, z: 4, core: 2. Of those that a mesh axis runs over, the one named last changes fastest.
Arguments:
- tiles: bfloat16 [6144, 128, 128], P(('gx', 'gy')), may hold values from -6 to 6
- tile_rows: int32 [6144], P(('gx', 'gy')), may hold values from 0 to 63, as said below
- tile_cols: int32 [6144], P(('gx', 'gy')), may hold values from 0 to 255
- tile_counts: int32 [32], P(('gx', 'gy')), may hold values from 48 to 192
- block_order: int32 [256], replicated, may hold values from 0 to 255, each once
- sketch: bfloat16 [32768, 128], replicated, may hold values from -6 to 6
Outputs:
- cell_factor: bfloat16 [262144, 128], P(('gx', 'gy'))
- gene_factor: float32 [32768, 128], P(('gx', 'gy'))
The draws below stay inside these ranges and needn't reach their ends.
Inputs may be any that keep to these rules, and one draw needn't show every extreme that they name: On each device the live slots (those below its count) hold distinct coordinate pairs (tile_rows, tile_cols) in increasing lexicographic order; later slots are unused. `block_order`: device d along gx+gy owns the gene blocks in entries d * 8 to (d + 1) * 8 - 1.
All inputs are finite; a program needn't handle non-finite values.
Results may differ from the reference program's by a relative error of at most 0.0019.
Values sent between devices are 32-bit elements; how exact they have to be, the bound alone decides.
No kernel may reach another device: no remote copies, remote signals or barrier semaphores. Data moves between devices by JAX's collectives and lax.ppermute only.
A program may use at most 192 MiB of HBM per device.

```python
import math
import jax
import jax.numpy as jnp
from jax import lax

TILE = 128
SKETCH = 128
GENES = 32768
CB_DEV = 64
TILES_DEV = 192
GENE_BLOCKS = 256
CELLS = 262144
ALL_TILES = 6144
DEVICES = 32


def tile_layout(key):
    base = jax.random.fold_in(key, 11)
    blocks_total = GENES // TILE
    device_ids = jnp.arange(DEVICES, dtype=jnp.int32)
    lowest = TILES_DEV // 3
    linear = lowest + (TILES_DEV - lowest) * device_ids // max(DEVICES - 1, 1)
    jitter = jax.random.randint(jax.random.fold_in(base, 1), (DEVICES,), -(TILES_DEV // 12), TILES_DEV // 12 + 1)
    counts = jnp.clip(linear + jitter, TILES_DEV // 4, TILES_DEV)
    fullest = jax.random.randint(jax.random.fold_in(base, 2), (), 3 * DEVICES // 4, DEVICES)
    counts = jnp.where(device_ids == fullest, TILES_DEV, counts).astype(jnp.int32)
    device_keys = jax.random.split(jax.random.fold_in(base, 3), DEVICES)
    offset = CB_DEV * blocks_total

    def one_device(device_key, live_count):
        codes = jax.random.permutation(device_key, offset)[:TILES_DEV].astype(jnp.int32)
        slots = jnp.arange(TILES_DEV, dtype=jnp.int32)
        shifted = jnp.where(slots < live_count, codes, codes + offset)
        ordered = jnp.sort(shifted)
        return jnp.where(ordered >= offset, ordered - offset, ordered)
    codes = jax.vmap(one_device)(device_keys, counts)
    return (counts, codes.reshape(-1))


def draw_tile_counts(key, part):
    return tile_layout(key)[0]


def draw_tile_rows(key, part):
    return (tile_layout(key)[1] // (GENES // TILE)).astype(jnp.int32)


def draw_tile_cols(key, part):
    return (tile_layout(key)[1] % (GENES // TILE)).astype(jnp.int32)


def shard_levels(own_key, dims, cuts, low, largest):
    loudness = 1.0
    for axis_at, parts in cuts:
        heights = jax.random.uniform(jax.random.fold_in(jax.random.fold_in(own_key, 6), axis_at), (parts,), jnp.float32, low / len(cuts), largest / len(cuts))
        loudness = loudness * jnp.repeat(jnp.exp(heights), dims[axis_at] // parts).reshape((-1,) + (1,) * (len(dims) - 1 - axis_at))
    return loudness


def noise(own_key, dims, deviation, bound, cuts=(), held_as=jnp.bfloat16):
    values = deviation * jax.random.normal(own_key, dims, jnp.float32)
    if cuts:
        values = values * shard_levels(own_key, dims, cuts, -0.22, 0.18)
    return jnp.clip(values, -bound, bound).astype(held_as)


def setup_inputs(seed: int = 0) -> dict:
    streams_of = jax.random.split(jax.random.key(seed), 7)
    return {
        "tiles": noise(streams_of[0], (ALL_TILES, TILE, TILE), 1.0, 6.0, ((0, 32),)),
        "tile_rows": draw_tile_rows(jax.random.fold_in(streams_of[6], 71), 0),
        "tile_cols": draw_tile_cols(jax.random.fold_in(streams_of[6], 71), 0),
        "tile_counts": draw_tile_counts(jax.random.fold_in(streams_of[6], 71), 0),
        "block_order": jax.random.permutation(streams_of[4], GENE_BLOCKS).astype(jnp.int32),
        "sketch": noise(streams_of[5], (GENES, SKETCH), 1.0, 6.0),
    }


def reference(tiles, tile_rows, tile_cols, tile_counts, block_order, sketch):
    blocks_total = GENES // TILE
    tile_sets = tiles.reshape(DEVICES, TILES_DEV, TILE, TILE)
    row_sets = tile_rows.reshape(DEVICES, TILES_DEV)
    col_sets = tile_cols.reshape(DEVICES, TILES_DEV)
    alive = jnp.arange(TILES_DEV, dtype=jnp.int32)[None, :] < tile_counts[:, None]
    sketch_blocks = sketch.reshape(blocks_total, TILE, SKETCH).astype(jnp.float32)

    def cell_part(items):
        tile_block, row_block, col_block, live = items
        product = jnp.einsum('tij,tjs->tis', tile_block.astype(jnp.float32), sketch_blocks[col_block])
        product = jnp.where(live[:, None, None], product, 0.0)
        return jnp.zeros((CB_DEV, TILE, SKETCH), jnp.float32).at[row_block].add(product)
    cell_sum = lax.map(cell_part, (tile_sets, row_sets, col_sets, alive)).reshape(CELLS, SKETCH)
    gram = jnp.dot(cell_sum.T.astype(jnp.float32), cell_sum.astype(jnp.float32), precision=lax.Precision.HIGHEST, preferred_element_type=jnp.float32)
    lower = jnp.linalg.cholesky(gram)
    cell_factor = (math.sqrt(CELLS) * lax.linalg.triangular_solve(lower, cell_sum, left_side=False, lower=True, transpose_a=True)).astype(jnp.bfloat16)
    cell_sets = cell_factor.reshape(DEVICES, CB_DEV, TILE, SKETCH)

    def gene_part(total, items):
        tile_block, row_block, col_block, live, cell_blocks = items
        product = jnp.einsum('tji,tjs->tis', tile_block.astype(jnp.float32), cell_blocks[row_block].astype(jnp.float32))
        product = jnp.where(live[:, None, None], product, 0.0)
        return (total.at[col_block].add(product), None)
    gene_sum, unused = lax.scan(gene_part, jnp.zeros((blocks_total, TILE, SKETCH), jnp.float32), (tile_sets, row_sets, col_sets, alive, cell_sets))
    ordered = gene_sum[block_order].reshape(GENES, SKETCH)
    gram_genes = jnp.dot(ordered.T.astype(jnp.float32), ordered.astype(jnp.float32), precision=lax.Precision.HIGHEST, preferred_element_type=jnp.float32)
    lower_genes = jnp.linalg.cholesky(gram_genes)
    gene_factor = math.sqrt(GENES) * lax.linalg.triangular_solve(lower_genes, ordered, left_side=False, lower=True, transpose_a=True)
    return (cell_factor, gene_factor)
```

```python
import functools
import math

import jax
import jax.numpy as jnp
from jax import lax
from jax.experimental import pallas as pl
from jax.experimental.pallas import tpu as pltpu
from jax.sharding import PartitionSpec as P

GROUP = 16
QUAD = 4


def bit_orders(nx, ny):
    low = (ny - 1).bit_length()
    bits = list(range(low + (nx - 1).bit_length()))
    swapped = list(bits)
    if low >= 3:
        swapped[1], swapped[2] = swapped[2], swapped[1]
    return bits, swapped


def place_in(order, owner):
    place = 0
    for bit in order:
        place = place * 2 + ((owner >> bit) & 1)
    return place


def sparse_kernel(
    plan, rows, cols, count, order, tiles, sketch, *refs
):
    nx, ny, parts, orders = plan
    pieces = refs[: 2 * parts]
    y_out, gram_out = refs[2 * parts : 2 * parts + 2]
    sketch_v, tiles_v, y_v, split_v, sums_v, slots, sem_s, sem_t, sem_y, sem_p = refs[2 * parts + 2 :]
    slots_all, side = tiles_v.shape[0], tiles_v.shape[1]
    blocks = sketch_v.shape[0]
    devices = nx * ny
    owned = blocks // devices
    per_part = owned // parts
    groups = slots_all // GROUP
    load_s = pltpu.make_async_copy(sketch, sketch_v, sem_s)
    load_s.start()

    def load(g):
        at = pl.ds(g * GROUP, GROUP)
        return pltpu.make_async_copy(tiles.at[at], tiles_v.at[at], sem_t.at[g])

    for g in range(groups):
        load(g).start()
    live = count[0]
    me = lax.axis_index("gx") * ny + lax.axis_index("gy")
    mine = [place_in(o, me) for o in orders]
    for owner in range(devices):
        for part in range(parts):
            kind = part % 2
            place = (place_in(orders[kind], owner) ^ mine[kind]) * per_part + part * devices * per_part
            for j in range(per_part):
                slots[order[owner * owned + part * per_part + j]] = place + j
    y_v[...] = jnp.zeros_like(y_v)

    @pl.loop(0, blocks)
    def _(b):
        sums_v[b] = jnp.zeros(sums_v.shape[1:], jnp.float32)

    load_s.wait()

    @pl.loop(0, groups)
    def _(g):
        load(g).wait()
        turns = jnp.clip((live - g * GROUP + QUAD - 1) // QUAD, 0, GROUP // QUAD)

        @pl.loop(0, turns)
        def _(q):
            start = g * GROUP + q * QUAD
            products = []
            for u in range(QUAD):
                t = start + u
                product = jnp.dot(tiles_v[t], sketch_v[cols[t]], preferred_element_type=jnp.float32)
                products.append(jnp.where(t < live, product, 0.0))
            for u in range(QUAD):
                y_v[rows[start + u]] += products[u]

    save_y = pltpu.make_async_copy(y_v, y_out, sem_y)
    save_y.start()
    gram_out[...] = jnp.zeros_like(gram_out)

    @pl.loop(0, y_v.shape[0] // QUAD)
    def _(b):
        at = pl.ds(b * QUAD, QUAD)
        y = y_v[at]
        high = y.astype(jnp.bfloat16)
        low = (y - high.astype(jnp.float32)).astype(jnp.bfloat16)
        both = jnp.concatenate([high, low], axis=-1)
        split_v[at] = both
        both = both.reshape(QUAD * side, 2 * y.shape[-1])
        g = lax.dot_general(both, both, (((0,), (0,)), ((), ())), preferred_element_type=jnp.float32)
        n = y.shape[-1]
        gram_out[...] += g[:n, :n] + ((g[:n, n:] + g[n:, :n]) + g[n:, n:])

    @pl.loop(0, (live + QUAD - 1) // QUAD)
    def _(q):
        products = []
        for u in range(QUAD):
            t = q * QUAD + u
            product = lax.dot_general(
                tiles_v[t], split_v[rows[t]], (((0,), (0,)), ((), ())), preferred_element_type=jnp.float32
            )
            n = product.shape[-1] // 2
            products.append(jnp.where(t < live, product[:, :n] + product[:, n:], 0.0))
        for u in range(QUAD):
            sums_v[slots[cols[q * QUAD + u]]] += products[u]

    size = devices * per_part // 2
    saves = [
        pltpu.make_async_copy(sums_v.at[pl.ds(k * size, size)], pieces[k], sem_p.at[k]) for k in range(2 * parts)
    ]
    for s in saves:
        s.start()
    for s in saves:
        s.wait()
    save_y.wait()


def on_device(tiles, tile_rows, tile_cols, tile_counts, block_order, sketch, nx, ny):
    slots_all, side, _ = tiles.shape
    genes, wide = sketch.shape
    blocks = genes // side
    cell_blocks = 64
    devices = nx * ny
    owned = blocks // devices
    parts = min(4, owned)
    per_part = owned // parts
    orders = bit_orders(nx, ny)
    size = devices * per_part // 2
    smem = pl.BlockSpec(memory_space=pltpu.SMEM)
    anywhere = pl.BlockSpec(memory_space=pl.ANY)
    outs = pl.pallas_call(
        functools.partial(sparse_kernel, (nx, ny, parts, orders)),
        out_shape=[jax.ShapeDtypeStruct((size, side, wide), jnp.float32)] * (2 * parts)
        + [
            jax.ShapeDtypeStruct((cell_blocks, side, wide), jnp.float32),
            jax.ShapeDtypeStruct((wide, wide), jnp.float32),
        ],
        in_specs=[smem] * 4 + [anywhere] * 2,
        out_specs=[anywhere] * (2 * parts + 1) + [pl.BlockSpec(memory_space=pltpu.VMEM)],
        scratch_shapes=[
            pltpu.VMEM((blocks, side, wide), jnp.bfloat16),
            pltpu.VMEM((slots_all, side, side), jnp.bfloat16),
            pltpu.VMEM((cell_blocks, side, wide), jnp.float32),
            pltpu.VMEM((cell_blocks, side, 2 * wide), jnp.bfloat16),
            pltpu.VMEM((blocks, side, wide), jnp.float32),
            pltpu.SMEM((blocks,), jnp.int32),
            pltpu.SemaphoreType.DMA,
            pltpu.SemaphoreType.DMA((slots_all // GROUP,)),
            pltpu.SemaphoreType.DMA,
            pltpu.SemaphoreType.DMA((2 * parts,)),
        ],
        compiler_params=pltpu.CompilerParams(vmem_limit_bytes=60 * 2**20),
        name="tile_products",
    )(tile_rows, tile_cols, tile_counts, block_order, tiles, sketch.reshape(blocks, side, wide))
    pieces, cell_sum, local_gram = outs[: 2 * parts], outs[-2], outs[-1]

    def swap(value, bit):
        partner = 1 << bit
        if partner < ny:
            return lax.ppermute(value, "gy", [(i, i ^ partner) for i in range(ny)])
        partner //= ny
        return lax.ppermute(value, "gx", [(i, i ^ partner) for i in range(nx)])

    def sum_all(value):
        for bit in orders[0]:
            value = value + swap(value, bit)
        return value

    def total(terms):
        return functools.reduce(jnp.add, terms)

    state = []
    for part in range(parts):
        state.append([pieces[2 * part], swap(pieces[2 * part + 1], orders[part % 2][0])])
    for step in range(1, len(orders[0])):
        for part in range(parts):
            terms = state[part]
            half = terms[0].shape[0] // 2
            arrived = swap(total([t[half:] for t in terms]), orders[part % 2][step])
            state[part] = [total([t[:half] for t in terms]), arrived]
    raw = jnp.concatenate([total(terms) for terms in state], axis=0).reshape(owned * side, wide)

    exact = lax.Precision.HIGHEST
    eye = jnp.eye(wide, dtype=jnp.float32)

    def inverse_of_factor(gram):
        lower = jnp.linalg.cholesky(gram)
        return lax.linalg.triangular_solve(lower, eye, left_side=True, lower=True)

    cells_all = cell_blocks * side * devices
    inverse = math.sqrt(cells_all) * inverse_of_factor(sum_all(local_gram))
    cell_factor = lax.dot_general(
        cell_sum.reshape(cell_blocks * side, wide), inverse, (((1,), (1,)), ((), ())), precision=exact
    ).astype(jnp.bfloat16)
    z = lax.dot_general(raw, inverse, (((1,), (1,)), ((), ())), precision=exact)
    gene_gram = sum_all(lax.dot_general(z, z, (((0,), (0,)), ((), ())), precision=exact))
    inverse_genes = math.sqrt(genes) * inverse_of_factor(gene_gram)
    gene_factor = lax.dot_general(z, inverse_genes, (((1,), (1,)), ((), ())), precision=exact)
    return (cell_factor, gene_factor)


def solution(mesh):
    placed = (
        P(("gx", "gy"), None, None),
        P(("gx", "gy")),
        P(("gx", "gy")),
        P(("gx", "gy")),
        P(),
        P(),
    )
    return jax.shard_map(
        functools.partial(on_device, nx=mesh.shape["gx"], ny=mesh.shape["gy"]),
        mesh=mesh,
        in_specs=placed,
        out_specs=(P(("gx", "gy"), None), P(("gx", "gy"), None)),
        check_vma=False,
    )
```

```python
import functools
import math

import jax
import jax.numpy as jnp
from jax import lax
from jax.experimental import pallas as pl
from jax.experimental.pallas import tpu as pltpu
from jax.sharding import PartitionSpec as P

GROUP = 16
PANEL = 32
EXACT = lax.Precision.HIGHEST
SMEM = pl.BlockSpec(memory_space=pltpu.SMEM)
VMEM = pl.BlockSpec(memory_space=pltpu.VMEM)
ANY = pl.BlockSpec(memory_space=pl.ANY)
ROOMY = pltpu.CompilerParams(vmem_limit_bytes=60 * 2**20)
CELL_BLOCKS = 64


def bit_orders(nx, ny, far_first=False):
    low = (ny - 1).bit_length()
    near, far = list(range(low)), list(range(low, low + (nx - 1).bit_length()))
    swapped = list(near)
    if low >= 3:
        swapped[1], swapped[2] = swapped[2], swapped[1]
    if far_first:
        return [o[:1] + far + o[1:] for o in (near, swapped)]
    return [o + far for o in (near, swapped)]


def place_in(order, owner):
    place = 0
    for bit in order:
        place = place * 2 + ((owner >> bit) & 1)
    return place


def pair_table(owned):
    if owned % 8:
        return [(0, owned // 2, False)]
    return [(0, owned // 4, False), (owned // 2, owned // 8, True), (3 * owned // 4, owned // 8, False)]


def list_tiles(nx, ny, pairs, owned, rows, cols, live, order, slots, list_row, list_tile, list_slot):
    devices = nx * ny
    me = lax.axis_index("gx") * ny + lax.axis_index("gy")

    @pl.loop(0, slots.shape[0])
    def _(b):
        slots[b] = -1

    total = 0
    for first, each, far_first in pairs:
        size = devices * each // 2
        for part, bits in enumerate(bit_orders(nx, ny, far_first)):
            mine = place_in(bits, me)
            for owner in range(devices):
                place = (place_in(bits, owner) ^ mine) * each
                place += jnp.where(place < size, 0, size) + part * size + total
                for j in range(each):
                    slots[order[owner * owned + first + part * each + j]] = place + j
        total += 4 * size

    def step(t, found):
        slot = slots[cols[t]]
        list_tile[found] = t
        list_row[found] = rows[t]
        list_slot[found] = slot
        return found + (slot >= 0).astype(jnp.int32)

    found = lax.fori_loop(0, live, step, jnp.int32(0))
    for u in range(GROUP):
        list_tile[found + u] = 0
        list_row[found + u] = 0
        list_slot[found + u] = total
    return found


def add_products(found, list_row, list_tile, list_slot, tiles_v, split_v, sums_v):
    @pl.loop(0, (found + GROUP - 1) // GROUP)
    def _(q):
        products = []
        for u in range(GROUP):
            k = q * GROUP + u
            product = lax.dot_general(
                tiles_v[list_tile[k]],
                split_v[list_row[k]],
                (((0,), (0,)), ((), ())),
                preferred_element_type=jnp.float32,
            )
            n = product.shape[-1] // 2
            products.append(product[:, :n] + product[:, n:])
        for u in range(GROUP):
            sums_v[list_slot[q * GROUP + u]] += products[u]


def zero(ref):
    @pl.loop(0, ref.shape[0])
    def _(b):
        ref[b] = jnp.zeros(ref.shape[1:], ref.dtype)


def save_pieces(pairs, sums_v, pieces, sem):
    saves = []
    base = 0
    for p in range(len(pairs)):
        size = pieces[8 * p].shape[0]
        for k in (5, 7, 4, 6, 1, 3, 0, 2):
            at = pl.ds(base + k * size, size)
            to = pieces[8 * p + k].at[pl.ds(0, size)]
            saves.append(pltpu.make_async_copy(sums_v.at[at], to, sem.at[8 * p + k]))
        base += 8 * size
    for s in saves:
        s.start()
    return saves


def first_kernel(nx, ny, pairs, owned, rows, cols, count, order, tiles, sketch, *refs):
    n_pieces = 8 * len(pairs)
    pieces, split_out = refs[:n_pieces], refs[n_pieces]
    (
        sketch_v, tiles_v, y_v, split_v, sums_v, gram_v, slots, list_row, list_tile, list_slot,
        sem_s, sem_t, sem_y, sem_p, sem_g,
    ) = refs[n_pieces + 1 :]
    cell_blocks = split_v.shape[0]
    live = count[0]
    groups = (live + GROUP - 1) // GROUP

    def load_tiles(g):
        at = pl.ds(g * GROUP, GROUP)
        return pltpu.make_async_copy(tiles.at[at], tiles_v.at[at], sem_t.at[g])

    @pl.loop(0, groups)
    def _(g):
        load_tiles(g).start()
        for u in range(GROUP):
            t = g * GROUP + u
            pltpu.make_async_copy(sketch.at[cols[t]], sketch_v.at[t], sem_s.at[g]).start()

    zero(y_v)
    zero(sums_v)
    found = list_tiles(nx, ny, pairs, owned, rows, cols, live, order, slots, list_row, list_tile, list_slot)

    @pl.loop(0, groups)
    def _(g):
        load_tiles(g).wait()
        at = pl.ds(g * GROUP, GROUP)
        pltpu.make_async_copy(sketch.at[pl.ds(0, GROUP)], sketch_v.at[at], sem_s.at[g]).wait()
        products = []
        for u in range(GROUP):
            t = g * GROUP + u
            products.append(jnp.dot(tiles_v[t], sketch_v[t], preferred_element_type=jnp.float32))
        for u in range(GROUP):
            t = g * GROUP + u
            y_v[jnp.where(t < live, rows[t], cell_blocks)] += products[u]

    gram_v[...] = jnp.zeros_like(gram_v)

    @pl.loop(0, cell_blocks // 8)
    def _(b):
        at = pl.ds(b * 8, 8)
        y = y_v[at]
        high = y.astype(jnp.bfloat16)
        low = (y - high.astype(jnp.float32)).astype(jnp.bfloat16)
        both = jnp.concatenate([high, low], axis=-1)
        split_v[at] = both
        rows = y.shape[0] * y.shape[1]
        gram_v[0] += lax.dot_general(
            high.reshape(rows, -1), both.reshape(rows, -1), (((0,), (0,)), ((), ())), preferred_element_type=jnp.float32
        )

    save_split = pltpu.make_async_copy(split_v, split_out, sem_y)
    save_split.start()
    n = y_v.shape[-1]
    cross = gram_v[0, :, n:]
    gram_v[0, :, :n] += cross + cross.T
    rider = pieces[5]
    save_gram = pltpu.make_async_copy(gram_v.at[:, :, pl.ds(0, n)], rider.at[pl.ds(rider.shape[0] - 1, 1)], sem_g)
    save_gram.start()
    add_products(found, list_row, list_tile, list_slot, tiles_v, split_v, sums_v)
    for s in save_pieces(pairs, sums_v, pieces, sem_p):
        s.wait()
    save_split.wait()
    save_gram.wait()


def second_kernel(nx, ny, pairs, owned, rows, cols, count, order, tiles, split, *refs):
    pieces = refs[: 8 * len(pairs)]
    tiles_v, split_v, sums_v, slots, list_row, list_tile, list_slot, sem_t, sem_y, sem_p = refs[8 * len(pairs) :]
    live = count[0]
    load_split = pltpu.make_async_copy(split, split_v, sem_y)
    load_tiles = pltpu.make_async_copy(tiles, tiles_v, sem_t)
    load_split.start()
    load_tiles.start()
    zero(sums_v)
    found = list_tiles(nx, ny, pairs, owned, rows, cols, live, order, slots, list_row, list_tile, list_slot)
    load_split.wait()
    load_tiles.wait()
    add_products(found, list_row, list_tile, list_slot, tiles_v, split_v, sums_v)
    for s in save_pieces(pairs, sums_v, pieces, sem_p):
        s.wait()


def combine_kernel(counts, *refs):
    out = refs[-1]
    first = row = 0
    for terms, size in counts:
        total = refs[first][...]
        for k in range(1, terms):
            total += refs[first + k][...]
        out[pl.ds(row, size)] = total
        first += terms
        row += size


def inverse_factor(gram):
    n = gram.shape[0]
    row = lax.broadcasted_iota(jnp.int32, (PANEL, n), 0)
    eye = lax.broadcasted_iota(jnp.int32, (n, n), 0) == lax.broadcasted_iota(jnp.int32, (n, n), 1)
    rest = jnp.concatenate([gram, eye.astype(jnp.float32)], axis=1)
    done = []
    for p in range(0, n, PANEL):
        a, w = rest[:PANEL, :n], rest[:PANEL, n:]
        columns = [jnp.broadcast_to(a[:, p + t : p + t + 1], (PANEL, n)) for t in range(PANEL)]
        scale = jnp.zeros((PANEL, n), jnp.float32)
        for s in range(PANEL):
            pivot = columns[s][s : s + 1]
            scale = jnp.where(row == s, lax.rsqrt(pivot), scale)
            if s + 1 < PANEL:
                factor = jnp.where(row > s, columns[s] * (1.0 / pivot), 0.0)
                for t in range(s + 1, PANEL):
                    columns[t] = columns[t] - factor * columns[t][s : s + 1]
                a = a - factor * a[s : s + 1]
                w = w - factor * w[s : s + 1]
        a, w = a * scale, w * scale
        done.append(w)
        if p + PANEL < n:
            update = lax.dot_general(
                a, jnp.concatenate([a, w], axis=1), (((0,), (0,)), ((), ())),
                precision=EXACT, preferred_element_type=jnp.float32,
            )
            rest = rest[PANEL:] - update[p + PANEL :]
    return jnp.concatenate(done, axis=0)


def times_transposed(x, w):
    return lax.dot_general(x, w, (((1,), (1,)), ((), ())), precision=EXACT, preferred_element_type=jnp.float32)


def factor_kernel(scale, gram, out):
    out[...] = inverse_factor(gram[...]) * scale


def cell_kernel(inverse, split, out):
    w = inverse[...]
    high = w.astype(jnp.bfloat16)
    low = (w - high.astype(jnp.float32)).astype(jnp.bfloat16)
    y = split[...].reshape(out.shape[0], -1)
    n = w.shape[0]

    def product(a, b):
        return lax.dot_general(a, b, (((1,), (1,)), ((), ())), preferred_element_type=jnp.float32)

    both = product(y, jnp.concatenate([high, high], axis=1))
    out[...] = (both + product(y[:, :n], low)).astype(out.dtype)


def owned_kernel(inverse, *refs):
    terms, (z_out, gram_out) = refs[:-2], refs[-2:]
    w = inverse[...]
    gram = None
    at = 0
    for term in terms:
        raw = term[...].reshape(-1, term.shape[-1])
        z = times_transposed(raw, w)
        z_out[pl.ds(at, raw.shape[0]), :] = z
        at += raw.shape[0]
        g = lax.dot_general(z, z, (((0,), (0,)), ((), ())), precision=EXACT, preferred_element_type=jnp.float32)
        gram = g if gram is None else gram + g
    gram_out[...] = gram


def gene_kernel(scale, gram, z, out):
    out[...] = times_transposed(z[...], inverse_factor(gram[...]) * scale)


def cost(microseconds):
    return pl.CostEstimate(flops=int(microseconds * 1e9), bytes_accessed=int(microseconds * 3e6), transcendentals=0)


def on_device(tiles, tile_rows, tile_cols, tile_counts, block_order, sketch, nx, ny):
    slots_all, side, _ = tiles.shape
    genes, wide = sketch.shape
    blocks = genes // side
    devices = nx * ny
    owned = blocks // devices
    table = pair_table(owned)
    orders = bit_orders(nx, ny)
    early_pairs, late_pairs = table[:2], table[2:]
    f32, bf16 = jnp.float32, jnp.bfloat16

    def piece_shapes(pairs, rider):
        sizes = [devices * each // 4 for _, each, _ in pairs for _ in range(8)]
        sizes[5] += rider
        return [jax.ShapeDtypeStruct((n, side, wide), f32) for n in sizes]

    def list_scratch():
        room = slots_all + GROUP
        return [pltpu.SMEM((blocks,), jnp.int32)] + [pltpu.SMEM((room,), jnp.int32)] * 3

    def sums_scratch(pairs):
        return pltpu.VMEM((sum(2 * each for _, each, _ in pairs) * devices + 1, side, wide), f32)

    def swap(value, bit):
        partner = 1 << bit
        if partner < ny:
            return lax.ppermute(value, "gy", [(i, i ^ partner) for i in range(ny)])
        partner //= ny
        return lax.ppermute(value, "gx", [(i, i ^ partner) for i in range(nx)])

    *early, split = pl.pallas_call(
        functools.partial(first_kernel, nx, ny, early_pairs, owned),
        out_shape=piece_shapes(early_pairs, 1)
        + [jax.ShapeDtypeStruct((CELL_BLOCKS, side, 2 * wide), bf16)],
        in_specs=[SMEM] * 4 + [ANY] * 2,
        out_specs=[ANY] * (8 * len(early_pairs) + 1),
        scratch_shapes=[
            pltpu.VMEM((slots_all, side, wide), bf16),
            pltpu.VMEM((slots_all, side, side), bf16),
            pltpu.VMEM((CELL_BLOCKS + 1, side, wide), f32),
            pltpu.VMEM((CELL_BLOCKS, side, 2 * wide), bf16),
            sums_scratch(early_pairs),
            pltpu.VMEM((1, wide, 2 * wide), f32),
            *list_scratch(),
            pltpu.SemaphoreType.DMA((slots_all // GROUP,)),
            pltpu.SemaphoreType.DMA((slots_all // GROUP,)),
            pltpu.SemaphoreType.DMA,
            pltpu.SemaphoreType.DMA((8 * len(early_pairs),)),
            pltpu.SemaphoreType.DMA,
        ],
        compiler_params=ROOMY,
        cost_estimate=cost(4.0),
        name="tile_products",
    )(tile_rows, tile_cols, tile_counts, block_order, tiles, sketch.reshape(blocks, side, wide))

    done_before = [tile_counts]

    def follows(value):
        return lax.optimization_barrier((value, done_before[0]))[0]

    def note(value):
        done_before[0] = value
        return value

    bits = orders[0]
    shared = next(k for k in range(1, len(bits)) if all(o[k:] == bits[k:] for o in orders))
    orders_of = [bit_orders(nx, ny, far_first) for _, _, far_first in table]
    state = {}

    def begin(pair, *arrays):
        kept, quarters = arrays[:4], arrays[4:]
        half = kept[0].shape[0]
        got = {k: swap(quarters[k], bits[0]) for k in (1, 3, 0, 2)}
        terms = [[[(kept[2 * part + upper], 0), (got[2 * part + upper], 0)] for upper in range(2)] for part in range(2)]
        rider = [(quarters[1], half), (got[1], half)] if quarters[1].shape[0] > half else []
        state[pair] = [1, half, terms, rider]

    def wait(pairs):
        found = []
        for pair in pairs:
            _, _, terms, rider = state[pair]
            for array, _ in [terms[part][1][-1] for part in range(2)] + rider[-1:]:
                if not any(array is f for f in found):
                    found.append(array)
        ready = lax.optimization_barrier((*found, done_before[0]))

        def swapped(term):
            return next(((r, term[1]) for f, r in zip(found, ready) if f is term[0]), term)

        for pair in pairs:
            step, size, terms, rider = state[pair]
            terms = [[[swapped(t) for t in upper] for upper in part] for part in terms]
            state[pair] = [step, size, terms, [swapped(t) for t in rider]]

    def combine(groups):
        counts = tuple((len(terms), size) for terms, size in groups)
        specs, arrays = [], []
        for terms, size in groups:
            for array, at in terms:
                specs.append(pl.BlockSpec((size, side, wide), functools.partial(lambda place, _: (place, 0, 0), at // size)))
                arrays.append(array)
        rows = sum(size for _, size in groups)
        return pl.pallas_call(
            functools.partial(combine_kernel, counts),
            grid=(1,),
            out_shape=jax.ShapeDtypeStruct((rows, side, wide), f32),
            in_specs=specs,
            out_specs=pl.BlockSpec((rows, side, wide), lambda _: (0, 0, 0)),
            compiler_params=pltpu.CompilerParams(vmem_limit_bytes=24 * 2**20),
            cost_estimate=cost(0.01),
            name="combine",
        )(*arrays)

    def halves(size, base, got):
        cut = size // 2
        return [[(array, at + upper * cut) for array, at in (base, got)] for upper in range(2)]

    def send_apart(pair):
        step, size, terms, rider = state[pair]
        sent = [combine([(terms[part][1], size)] + ([(rider, 1)] if rider and part == 0 else [])) for part in range(2)]
        got = [swap(note(sent[part]), orders_of[pair][part][step]) for part in range(2)]
        base = [combine([(terms[part][0], size)]) for part in range(2)]
        rider = [(sent[0], size), (got[0], size)] if rider else []
        state[pair] = [step + 1, size // 2, [halves(size, (base[part], 0), (got[part], 0)) for part in range(2)], rider]

    def send_both(pair):
        step, size, terms, rider = state[pair]
        sent = note(combine([(terms[part][1], size) for part in range(2)] + ([(rider, 1)] if rider else [])))
        got = swap(sent, orders_of[pair][0][step])
        base = combine([(terms[part][0], size) for part in range(2)])
        rider = [(sent, 2 * size), (got, 2 * size)] if rider else []
        state[pair] = [step + 1, size // 2, [halves(size, (base, part * size), (got, part * size)) for part in range(2)], rider]

    def finish(pair):
        _, size, terms, _ = state[pair]
        return combine([(terms[part][0], max(1, 2 * size)) for part in range(2)])

    def small_sum(pair):
        return functools.reduce(jnp.add, [array[at] for array, at in state[pair][3]])

    cells_all = CELL_BLOCKS * side * devices

    def late_products(pairs):
        return pl.pallas_call(
            functools.partial(second_kernel, nx, ny, pairs, owned),
            out_shape=piece_shapes(pairs, 0),
            in_specs=[SMEM] * 4 + [ANY] * 2,
            out_specs=[ANY] * (8 * len(pairs)),
            scratch_shapes=[
                pltpu.VMEM((slots_all, side, side), bf16),
                pltpu.VMEM((CELL_BLOCKS, side, 2 * wide), bf16),
                sums_scratch(pairs),
                *list_scratch(),
                pltpu.SemaphoreType.DMA,
                pltpu.SemaphoreType.DMA,
                pltpu.SemaphoreType.DMA((8 * len(pairs),)),
            ],
            compiler_params=pltpu.CompilerParams(vmem_limit_bytes=36 * 2**20),
            cost_estimate=cost(4.0),
            name="late_products",
        )(tile_rows, tile_cols, tile_counts, block_order, tiles, follows(split))

    def cell_inverse(gram):
        return note(
            pl.pallas_call(
                functools.partial(factor_kernel, math.sqrt(cells_all)),
                out_shape=jax.ShapeDtypeStruct((wide, wide), f32),
                in_specs=[VMEM],
                out_specs=VMEM,
                cost_estimate=cost(1.5),
                name="cell_cholesky",
            )(follows(gram))
        )

    def cells(inverse):
        step = 8
        return note(
            pl.pallas_call(
                cell_kernel,
                grid=(CELL_BLOCKS // step,),
                out_shape=jax.ShapeDtypeStruct((CELL_BLOCKS * side, wide), bf16),
                in_specs=[
                    pl.BlockSpec((wide, wide), lambda b: (0, 0)),
                    pl.BlockSpec((step, side, 2 * wide), lambda b: (b, 0, 0)),
                ],
                out_specs=pl.BlockSpec((step * side, wide), lambda b: (b, 0)),
                cost_estimate=cost(1.0),
                name="cell_factor",
            )(follows(inverse), split)
        )

    begin(0, *early[:8])
    if len(table) == 1:
        for step in range(1, len(bits)):
            wait([0])
            send_apart(0) if step < shared else send_both(0)
        wait([0])
        inverse = cell_inverse(small_sum(0))
        finals = [finish(0)]
        cell_factor = cells(inverse)
    else:
        begin(1, *early[8:])
        wait([0])
        send_apart(0)
        wait([1])
        send_both(1)
        late = late_products(late_pairs)
        note(late[0])
        begin(2, *late)
        wait([0, 1])
        send_apart(0)
        send_both(1)
        wait([2])
        send_apart(2)
        wait([0, 1, 2])
        send_both(0)
        send_apart(2)
        send_apart(1)
        wait([0, 1, 2])
        send_both(0)
        send_both(2)
        send_apart(1)
        wait([0, 1, 2])
        send_both(2)
        inverse = cell_inverse(small_sum(0))
        finals = [finish(0), finish(1)]
        cell_factor = cells(inverse)
        wait([2])
        finals.append(finish(2))
    z, gene_gram = pl.pallas_call(
        owned_kernel,
        out_shape=[jax.ShapeDtypeStruct((owned * side, wide), f32), jax.ShapeDtypeStruct((wide, wide), f32)],
        in_specs=[VMEM] * (1 + len(finals)),
        out_specs=[VMEM] * 2,
        name="gene_gram",
    )(inverse, *finals)
    for bit in bits:
        gene_gram = gene_gram + swap(gene_gram, bit)
    gene_factor = pl.pallas_call(
        functools.partial(gene_kernel, math.sqrt(genes)),
        out_shape=jax.ShapeDtypeStruct((owned * side, wide), f32),
        in_specs=[VMEM] * 2,
        out_specs=VMEM,
        name="gene_factor",
    )(gene_gram, z)
    return (cell_factor, gene_factor)


def solution(mesh):
    placed = (
        P(("gx", "gy"), None, None),
        P(("gx", "gy")),
        P(("gx", "gy")),
        P(("gx", "gy")),
        P(),
        P(),
    )
    return jax.shard_map(
        functools.partial(on_device, nx=mesh.shape["gx"], ny=mesh.shape["gy"]),
        mesh=mesh,
        in_specs=placed,
        out_specs=(P(("gx", "gy"), None), P(("gx", "gy"), None)),
        check_vma=False,
    )
```

```python
import functools
import math

import jax
import jax.numpy as jnp
from jax import lax
from jax.experimental import pallas as pl
from jax.experimental.pallas import tpu as pltpu
from jax.sharding import PartitionSpec as P

GROUP = 16
PANEL = 32
EXACT = lax.Precision.HIGHEST
SMEM = pl.BlockSpec(memory_space=pltpu.SMEM)
VMEM = pl.BlockSpec(memory_space=pltpu.VMEM)
ANY = pl.BlockSpec(memory_space=pl.ANY)
ROOMY = pltpu.CompilerParams(vmem_limit_bytes=60 * 2**20)
CELL_BLOCKS = 64


def bit_orders(nx, ny, far_first=False):
    low = (ny - 1).bit_length()
    near, far = list(range(low)), list(range(low, low + (nx - 1).bit_length()))
    swapped = list(near)
    if low >= 3:
        swapped[1], swapped[2] = swapped[2], swapped[1]
    if far_first:
        return [o[:1] + far + o[1:] for o in (near, swapped)]
    return [o + far for o in (near, swapped)]


def place_in(order, owner):
    place = 0
    for bit in order:
        place = place * 2 + ((owner >> bit) & 1)
    return place


def pair_table(owned):
    if owned % 8:
        return [(0, owned // 2, False)]
    return [(0, owned // 4, False), (owned // 2, owned // 8, True), (3 * owned // 4, owned // 8, False)]


def list_tiles(nx, ny, pairs, owned, rows, cols, live, order, slots, list_row, list_tile, list_slot):
    devices = nx * ny
    me = lax.axis_index("gx") * ny + lax.axis_index("gy")

    @pl.loop(0, slots.shape[0])
    def _(b):
        slots[b] = -1

    total = 0
    for first, each, far_first in pairs:
        size = devices * each // 2
        for part, bits in enumerate(bit_orders(nx, ny, far_first)):
            mine = place_in(bits, me)
            for owner in range(devices):
                place = (place_in(bits, owner) ^ mine) * each
                place += jnp.where(place < size, 0, size) + part * size + total
                for j in range(each):
                    slots[order[owner * owned + first + part * each + j]] = place + j
        total += 4 * size

    room = list_tile.shape[0] // len(pairs)
    ends = [sum(2 * e * devices for _, e, _ in pairs[: k + 1]) for k in range(len(pairs))]

    def step(t, found):
        slot = slots[cols[t]]
        row = rows[t]
        later = []
        for k in range(len(pairs)):
            at = found[k] + k * room
            list_tile[at] = t
            list_row[at] = row
            list_slot[at] = slot
            low = ends[k - 1] if k else 0
            later.append(found[k] + jnp.logical_and(slot >= low, slot < ends[k]).astype(jnp.int32))
        return tuple(later)

    found = lax.fori_loop(0, live, step, (jnp.int32(0),) * len(pairs))
    for k in range(len(pairs)):
        for u in range(GROUP):
            list_tile[found[k] + k * room + u] = 0
            list_row[found[k] + k * room + u] = 0
            list_slot[found[k] + k * room + u] = total
    return found


def add_products(found, first, list_row, list_tile, list_slot, tiles_v, split_v, sums_v):
    @pl.loop(0, (found + GROUP - 1) // GROUP)
    def _(q):
        products = []
        for u in range(GROUP):
            k = first + q * GROUP + u
            product = lax.dot_general(
                tiles_v[list_tile[k]],
                split_v[list_row[k]],
                (((0,), (0,)), ((), ())),
                preferred_element_type=jnp.float32,
            )
            n = product.shape[-1] // 2
            products.append(product[:, :n] + product[:, n:])
        for u in range(GROUP):
            sums_v[list_slot[first + q * GROUP + u]] += products[u]


def zero(ref):
    @pl.loop(0, ref.shape[0])
    def _(b):
        ref[b] = jnp.zeros(ref.shape[1:], ref.dtype)


def add_and_save(pairs, found, list_row, list_tile, list_slot, tiles_v, split_v, sums_v, pieces, sem):
    saves = []
    base = 0
    room = list_tile.shape[0] // len(pairs)
    for p in range(len(pairs)):
        add_products(found[p], p * room, list_row, list_tile, list_slot, tiles_v, split_v, sums_v)
        size = pieces[8 * p].shape[0]
        for k in (5, 7, 4, 6, 1, 3, 0, 2):
            at = pl.ds(base + k * size, size)
            to = pieces[8 * p + k].at[pl.ds(0, size)]
            saves.append(pltpu.make_async_copy(sums_v.at[at], to, sem.at[8 * p + k]))
            saves[-1].start()
        base += 8 * size
    for s in saves:
        s.wait()


def first_kernel(nx, ny, pairs, owned, rows, cols, count, order, tiles, sketch, *refs):
    n_pieces = 8 * len(pairs)
    pieces, split_out = refs[:n_pieces], refs[n_pieces]
    (
        sketch_v, tiles_v, y_v, split_v, sums_v, gram_v, slots, list_row, list_tile, list_slot,
        sem_s, sem_t, sem_y, sem_p, sem_g,
    ) = refs[n_pieces + 1 :]
    cell_blocks = split_v.shape[0]
    live = count[0]
    groups = (live + GROUP - 1) // GROUP

    def load_tiles(g):
        at = pl.ds(g * GROUP, GROUP)
        return pltpu.make_async_copy(tiles.at[at], tiles_v.at[at], sem_t.at[g])

    @pl.loop(0, groups)
    def _(g):
        load_tiles(g).start()
        for u in range(GROUP):
            t = g * GROUP + u
            pltpu.make_async_copy(sketch.at[cols[t]], sketch_v.at[t], sem_s.at[g]).start()

    zero(y_v)
    zero(sums_v)
    found = list_tiles(nx, ny, pairs, owned, rows, cols, live, order, slots, list_row, list_tile, list_slot)

    @pl.loop(0, groups)
    def _(g):
        load_tiles(g).wait()
        at = pl.ds(g * GROUP, GROUP)
        pltpu.make_async_copy(sketch.at[pl.ds(0, GROUP)], sketch_v.at[at], sem_s.at[g]).wait()
        products = []
        for u in range(GROUP):
            t = g * GROUP + u
            products.append(jnp.dot(tiles_v[t], sketch_v[t], preferred_element_type=jnp.float32))
        for u in range(GROUP):
            t = g * GROUP + u
            y_v[jnp.where(t < live, rows[t], cell_blocks)] += products[u]

    gram_v[...] = jnp.zeros_like(gram_v)

    @pl.loop(0, cell_blocks // 8)
    def _(b):
        at = pl.ds(b * 8, 8)
        y = y_v[at]
        high = y.astype(jnp.bfloat16)
        low = (y - high.astype(jnp.float32)).astype(jnp.bfloat16)
        both = jnp.concatenate([high, low], axis=-1)
        split_v[at] = both
        rows = y.shape[0] * y.shape[1]
        gram_v[0] += lax.dot_general(
            high.reshape(rows, -1), both.reshape(rows, -1), (((0,), (0,)), ((), ())), preferred_element_type=jnp.float32
        )

    save_split = pltpu.make_async_copy(split_v, split_out, sem_y)
    save_split.start()
    n = y_v.shape[-1]
    cross = gram_v[0, :, n:]
    gram_v[0, :, :n] += cross + cross.T
    rider = pieces[5]
    save_gram = pltpu.make_async_copy(gram_v.at[:, :, pl.ds(0, n)], rider.at[pl.ds(rider.shape[0] - 1, 1)], sem_g)
    save_gram.start()
    add_and_save(pairs, found, list_row, list_tile, list_slot, tiles_v, split_v, sums_v, pieces, sem_p)
    save_split.wait()
    save_gram.wait()


def second_kernel(nx, ny, pairs, owned, rows, cols, count, order, tiles, split, *refs):
    pieces = refs[: 8 * len(pairs)]
    tiles_v, split_v, sums_v, slots, list_row, list_tile, list_slot, sem_t, sem_y, sem_p = refs[8 * len(pairs) :]
    live = count[0]
    load_split = pltpu.make_async_copy(split, split_v, sem_y)
    load_tiles = pltpu.make_async_copy(tiles, tiles_v, sem_t)
    load_split.start()
    load_tiles.start()
    zero(sums_v)
    found = list_tiles(nx, ny, pairs, owned, rows, cols, live, order, slots, list_row, list_tile, list_slot)
    load_split.wait()
    load_tiles.wait()
    add_and_save(pairs, found, list_row, list_tile, list_slot, tiles_v, split_v, sums_v, pieces, sem_p)


def combine_kernel(counts, *refs):
    out = refs[-1]
    first = row = 0
    for terms, size in counts:
        total = refs[first][...]
        for k in range(1, terms):
            total += refs[first + k][...]
        out[pl.ds(row, size)] = total
        first += terms
        row += size


def inverse_factor(gram, beside=lambda panel: None):
    n = gram.shape[0]
    row = lax.broadcasted_iota(jnp.int32, (PANEL, n), 0)
    eye = lax.broadcasted_iota(jnp.int32, (n, n), 0) == lax.broadcasted_iota(jnp.int32, (n, n), 1)
    rest = jnp.concatenate([gram, eye.astype(jnp.float32)], axis=1)
    done = []
    for p in range(0, n, PANEL):
        a, w = rest[:PANEL, :n], rest[:PANEL, n:]
        columns = [jnp.broadcast_to(a[:, p + t : p + t + 1], (PANEL, n)) for t in range(PANEL)]
        scale = jnp.zeros((PANEL, n), jnp.float32)
        for s in range(PANEL):
            pivot = columns[s][s : s + 1]
            scale = jnp.where(row == s, lax.rsqrt(pivot), scale)
            if s + 1 < PANEL:
                factor = jnp.where(row > s, columns[s] * (1.0 / pivot), 0.0)
                for t in range(s + 1, PANEL):
                    columns[t] = columns[t] - factor * columns[t][s : s + 1]
                a = a - factor * a[s : s + 1]
                w = w - factor * w[s : s + 1]
        a, w = a * scale, w * scale
        done.append(w)
        beside(p // PANEL)
        if p + PANEL < n:
            update = lax.dot_general(
                a, jnp.concatenate([a, w], axis=1), (((0,), (0,)), ((), ())),
                precision=EXACT, preferred_element_type=jnp.float32,
            )
            rest = rest[PANEL:] - update[p + PANEL :]
    return jnp.concatenate(done, axis=0)


def times_transposed(x, w):
    return lax.dot_general(x, w, (((1,), (1,)), ((), ())), precision=EXACT, preferred_element_type=jnp.float32)


def total_of(refs):
    return functools.reduce(jnp.add, [r[...].reshape(r.shape[-2:]) for r in refs])


def factor_kernel(scale, *refs):
    gram, out = refs[:-1], refs[-1]
    out[...] = (inverse_factor(total_of(gram)) * scale).T


def owned_kernel(counts, has_gram, inverse, *refs):
    gram, terms, (z_out, gram_out) = refs[:has_gram], refs[has_gram:-2], refs[-2:]
    rows = []
    first = 0
    for k in counts:
        rows.append(functools.reduce(jnp.add, [t[...] for t in terms[first : first + k]]))
        first += k
    raw = jnp.concatenate(rows, axis=0) if len(rows) > 1 else rows[0]
    raw = raw.reshape(-1, raw.shape[-1])
    z = jnp.dot(raw, inverse[...], precision=EXACT, preferred_element_type=jnp.float32)
    z_out[...] = z
    g = lax.dot_general(z, z, (((0,), (0,)), ((), ())), precision=EXACT, preferred_element_type=jnp.float32)
    if has_gram:
        g += gram[0][0]
    gram_out[0] = g


def last_kernel(scale, n_grams, split, inverse, *refs):
    split_v, out_v, sem_in, sem_out = refs[-4:]
    grams, zs = refs[:n_grams], refs[n_grams:-6]
    out, cells = refs[-6:-4]
    chunks = sem_in.shape[0]
    blocks, side, both = split_v.shape
    chunk, n = blocks // chunks, both // 2
    rows = chunk * side
    loads, saves = [], []
    for c in range(chunks):
        at = pl.ds(c * chunk, chunk)
        loads.append(pltpu.make_async_copy(split.at[at], split_v.at[at], sem_in.at[c]))
        at = pl.ds(c * rows, rows)
        saves.append(pltpu.make_async_copy(out_v.at[at], cells.at[at], sem_out.at[c]))
        loads[c].start()
    high = inverse[...].astype(jnp.bfloat16)
    low = (inverse[...] - high.astype(jnp.float32)).astype(jnp.bfloat16)
    right = jnp.concatenate(
        [jnp.concatenate([high, low], axis=1), jnp.concatenate([high, jnp.zeros_like(low)], axis=1)], axis=0
    )

    def cell_rows(c):
        loads[c].wait()
        y = split_v[pl.ds(c * chunk, chunk)].reshape(rows, both)
        g = jnp.dot(y, right, preferred_element_type=jnp.float32)
        out_v[pl.ds(c * rows, rows), :] = (g[:, :n] + g[:, n:]).astype(out_v.dtype)
        saves[c].start()

    w = inverse_factor(total_of(grams), cell_rows) * scale
    at = 0
    for z in zs:
        out[pl.ds(at, z.shape[0]), :] = times_transposed(z[...], w)
        at += z.shape[0]
    for save in saves:
        save.wait()


def cost(microseconds):
    return pl.CostEstimate(flops=int(microseconds * 1e9), bytes_accessed=int(microseconds * 3e6), transcendentals=0)


def on_device(tiles, tile_rows, tile_cols, tile_counts, block_order, sketch, nx, ny):
    slots_all, side, _ = tiles.shape
    genes, wide = sketch.shape
    blocks = genes // side
    devices = nx * ny
    owned = blocks // devices
    table = pair_table(owned)
    orders = bit_orders(nx, ny)
    early_pairs, late_pairs = table[:2], table[2:]
    f32, bf16 = jnp.float32, jnp.bfloat16

    def piece_shapes(pairs, rider):
        sizes = [devices * each // 4 for _, each, _ in pairs for _ in range(8)]
        sizes[5] += rider
        return [jax.ShapeDtypeStruct((n, side, wide), f32) for n in sizes]

    def list_scratch(pairs):
        room = slots_all + GROUP
        return [pltpu.SMEM((blocks,), jnp.int32)] + [pltpu.SMEM((len(pairs) * room,), jnp.int32)] * 3

    def sums_scratch(pairs):
        return pltpu.VMEM((sum(2 * each for _, each, _ in pairs) * devices + 1, side, wide), f32)

    def swap(value, bit):
        partner = 1 << bit
        if partner < ny:
            return lax.ppermute(value, "gy", [(i, i ^ partner) for i in range(ny)])
        partner //= ny
        return lax.ppermute(value, "gx", [(i, i ^ partner) for i in range(nx)])

    *early, split = pl.pallas_call(
        functools.partial(first_kernel, nx, ny, early_pairs, owned),
        out_shape=piece_shapes(early_pairs, 1)
        + [jax.ShapeDtypeStruct((CELL_BLOCKS, side, 2 * wide), bf16)],
        in_specs=[SMEM] * 4 + [ANY] * 2,
        out_specs=[ANY] * (8 * len(early_pairs) + 1),
        scratch_shapes=[
            pltpu.VMEM((slots_all, side, wide), bf16),
            pltpu.VMEM((slots_all, side, side), bf16),
            pltpu.VMEM((CELL_BLOCKS + 1, side, wide), f32),
            pltpu.VMEM((CELL_BLOCKS, side, 2 * wide), bf16),
            sums_scratch(early_pairs),
            pltpu.VMEM((1, wide, 2 * wide), f32),
            *list_scratch(early_pairs),
            pltpu.SemaphoreType.DMA((slots_all // GROUP,)),
            pltpu.SemaphoreType.DMA((slots_all // GROUP,)),
            pltpu.SemaphoreType.DMA,
            pltpu.SemaphoreType.DMA((8 * len(early_pairs),)),
            pltpu.SemaphoreType.DMA,
        ],
        compiler_params=ROOMY,
        cost_estimate=cost(4.0),
        name="tile_products",
    )(tile_rows, tile_cols, tile_counts, block_order, tiles, sketch.reshape(blocks, side, wide))

    done_before = [tile_counts]

    def follows(value):
        return lax.optimization_barrier((value, done_before[0]))[0]

    def note(value):
        done_before[0] = value
        return value

    bits = orders[0]
    shared = next(k for k in range(1, len(bits)) if all(o[k:] == bits[k:] for o in orders))
    orders_of = [bit_orders(nx, ny, far_first) for _, _, far_first in table]
    state = {}

    def begin(pair, *arrays):
        kept, quarters = arrays[:4], arrays[4:]
        half = kept[0].shape[0]
        terms = [[[(kept[2 * part + upper], 0)] for upper in range(2)] for part in range(2)]
        state[pair] = [1, half, terms, []]
        if quarters[1].shape[0] > half:
            state[pair][3] = [(quarters[1], half)]

        for k in (1, 3, 0, 2):
            got = swap(quarters[k], orders_of[pair][0][0])
            terms[k // 2][k % 2].append((got, 0))
            if k == 1 and state[pair][3]:
                state[pair][3].append((got, half))

    def wait(pairs):
        found = []
        for pair in pairs:
            _, _, terms, rider = state[pair]
            for array, _ in [terms[part][1][-1] for part in range(2)] + rider[-1:]:
                if not any(array is f for f in found):
                    found.append(array)
        ready = lax.optimization_barrier((*found, done_before[0]))

        def swapped(term):
            return next(((r, term[1]) for f, r in zip(found, ready) if f is term[0]), term)

        for pair in pairs:
            step, size, terms, rider = state[pair]
            terms = [[[swapped(t) for t in upper] for upper in part] for part in terms]
            state[pair] = [step, size, terms, [swapped(t) for t in rider]]

    def combine(groups):
        counts = tuple((len(terms), size) for terms, size in groups)
        specs, arrays = [], []
        for terms, size in groups:
            for array, at in terms:
                specs.append(pl.BlockSpec((size, side, wide), functools.partial(lambda place, _: (place, 0, 0), at // size)))
                arrays.append(array)
        rows = sum(size for _, size in groups)
        return pl.pallas_call(
            functools.partial(combine_kernel, counts),
            grid=(1,),
            out_shape=jax.ShapeDtypeStruct((rows, side, wide), f32),
            in_specs=specs,
            out_specs=pl.BlockSpec((rows, side, wide), lambda _: (0, 0, 0)),
            compiler_params=pltpu.CompilerParams(vmem_limit_bytes=24 * 2**20),
            cost_estimate=cost(0.01),
            name="combine",
        )(*arrays)

    def halves(size, base, got):
        cut = size // 2
        return [[(array, at + upper * cut) for array, at in (base, got)] for upper in range(2)]

    def send_upper(pair, part):
        step, size, terms, rider = state[pair]
        groups = [(terms[part][1], size)] + ([(rider, 1)] if rider and part == 0 else [])
        sent = note(combine(groups))
        return sent, swap(sent, orders_of[pair][part][step])

    def keep_lower(pair, sent, got):
        step, size, terms, rider = state[pair]
        base = [combine([(terms[part][0], size)]) for part in range(2)]
        rider = [(sent[0], size), (got[0], size)] if rider else []
        state[pair] = [step + 1, size // 2, [halves(size, (base[part], 0), (got[part], 0)) for part in range(2)], rider]

    def send_apart(pair):
        moved = [send_upper(pair, part) for part in range(2)]
        keep_lower(pair, *zip(*moved))

    def send_both_upper(pair):
        step, size, terms, rider = state[pair]
        sent = note(combine([(terms[part][1], size) for part in range(2)] + ([(rider, 1)] if rider else [])))
        return sent, swap(sent, orders_of[pair][0][step])

    def keep_both_lower(pair, sent, got):
        step, size, terms, rider = state[pair]
        base = combine([(terms[part][0], size) for part in range(2)])
        rider = [(sent, 2 * size), (got, 2 * size)] if rider else []
        state[pair] = [step + 1, size // 2, [halves(size, (base, part * size), (got, part * size)) for part in range(2)], rider]

    def send_both(pair):
        keep_both_lower(pair, *send_both_upper(pair))

    def term_specs(groups):
        specs, arrays = [], []
        for terms, size in groups:
            for array, at in terms:
                specs.append(pl.BlockSpec((size, side, wide), functools.partial(lambda place, _: (place, 0, 0), at // size)))
                arrays.append(array)
        return specs, arrays

    def owners(pairs, inverse, gram=()):
        groups = [(state[p][2][part][0], max(1, 2 * state[p][1])) for p in pairs for part in range(2)]
        specs, arrays = term_specs(groups)
        rows = sum(size for _, size in groups) * side
        whole = pl.BlockSpec((wide, wide), lambda _: (0, 0))
        square = pl.BlockSpec((1, wide, wide), lambda _: (0, 0, 0))
        z, gram = pl.pallas_call(
            functools.partial(owned_kernel, [len(terms) for terms, _ in groups], len(gram)),
            grid=(1,),
            out_shape=[jax.ShapeDtypeStruct((rows, wide), f32), jax.ShapeDtypeStruct((1, wide, wide), f32)],
            in_specs=[whole] + [square] * len(gram) + specs,
            out_specs=[pl.BlockSpec((rows, wide), lambda _: (0, 0)), square],
            compiler_params=pltpu.CompilerParams(vmem_limit_bytes=24 * 2**20),
            cost_estimate=cost(0.5),
            name="owned_gram",
        )(inverse, *gram, *arrays)
        return z, note(gram)

    def small_terms(pair):
        return [array[at : at + 1] for array, at in state[pair][3]]

    cells_all = CELL_BLOCKS * side * devices

    def late_products(pairs):
        return pl.pallas_call(
            functools.partial(second_kernel, nx, ny, pairs, owned),
            out_shape=piece_shapes(pairs, 0),
            in_specs=[SMEM] * 4 + [ANY] * 2,
            out_specs=[ANY] * (8 * len(pairs)),
            scratch_shapes=[
                pltpu.VMEM((slots_all, side, side), bf16),
                pltpu.VMEM((CELL_BLOCKS, side, 2 * wide), bf16),
                sums_scratch(pairs),
                *list_scratch(pairs),
                pltpu.SemaphoreType.DMA,
                pltpu.SemaphoreType.DMA,
                pltpu.SemaphoreType.DMA((8 * len(pairs),)),
            ],
            compiler_params=pltpu.CompilerParams(vmem_limit_bytes=36 * 2**20),
            cost_estimate=cost(4.0),
            name="late_products",
        )(tile_rows, tile_cols, tile_counts, block_order, tiles, follows(split))

    def cell_inverse(*grams):
        return note(
            pl.pallas_call(
                functools.partial(factor_kernel, math.sqrt(cells_all)),
                out_shape=jax.ShapeDtypeStruct((wide, wide), f32),
                in_specs=[VMEM] * len(grams),
                out_specs=VMEM,
                cost_estimate=cost(1.5),
                name="cell_cholesky",
            )(follows(grams[0]), *grams[1:])
        )

    begin(0, *early[:8])
    if len(table) == 1:
        for step in range(1, len(bits)):
            wait([0])
            send_apart(0) if step < shared else send_both(0)
        wait([0])
        inverse = cell_inverse(*small_terms(0))
        zs, gene_gram = [None], None
        zs[0], gene_gram = owners([0], inverse)
    else:
        begin(1, *early[8:])
        wait([0])
        send_apart(0)
        wait([1])
        send_both(1)
        late = late_products(late_pairs)
        note(late[0])
        begin(2, *late)
        wait([0, 1])
        send_apart(0)
        send_both(1)
        wait([2])
        send_apart(2)
        wait([0, 1, 2])
        send_both(0)
        send_apart(2)
        send_apart(1)
        wait([0, 1, 2])
        send_both(0)
        send_both(2)
        send_apart(1)
        wait([0, 1, 2])
        send_both(2)
        inverse = cell_inverse(*small_terms(0))
        z_early, gene_gram = owners([0, 1], inverse)
        wait([2])
        z_late, gene_gram = owners([2], inverse, (gene_gram,))
        zs = [z_early, z_late]

    grams = [gene_gram]
    for k, bit in enumerate(bits):
        if k:
            grams = [combine([([(g, 0) for g in grams], 1)])]
        grams.append(swap(grams[0], bit))
    chunks = wide // PANEL
    gene_factor, cell_factor = pl.pallas_call(
        functools.partial(last_kernel, math.sqrt(genes), len(grams)),
        out_shape=[
            jax.ShapeDtypeStruct((owned * side, wide), f32),
            jax.ShapeDtypeStruct((CELL_BLOCKS * side, wide), bf16),
        ],
        in_specs=[ANY] + [VMEM] * (1 + len(grams) + len(zs)),
        out_specs=[VMEM, ANY],
        scratch_shapes=[
            pltpu.VMEM((CELL_BLOCKS, side, 2 * wide), bf16),
            pltpu.VMEM((CELL_BLOCKS * side, wide), bf16),
            pltpu.SemaphoreType.DMA((chunks,)),
            pltpu.SemaphoreType.DMA((chunks,)),
        ],
        compiler_params=ROOMY,
        name="factors",
    )(split, inverse, *grams, *zs)
    return (cell_factor, gene_factor)


def solution(mesh):
    placed = (
        P(("gx", "gy"), None, None),
        P(("gx", "gy")),
        P(("gx", "gy")),
        P(("gx", "gy")),
        P(),
        P(),
    )
    return jax.shard_map(
        functools.partial(on_device, nx=mesh.shape["gx"], ny=mesh.shape["gy"]),
        mesh=mesh,
        in_specs=placed,
        out_specs=(P(("gx", "gy"), None), P(("gx", "gy"), None)),
        check_vma=False,
    )
```

```python
import functools
import math

import jax
import jax.numpy as jnp
from jax import lax
from jax.experimental import pallas as pl
from jax.experimental.pallas import tpu as pltpu
from jax.sharding import PartitionSpec as P

GROUP = 16
PANEL = 32
EXACT = lax.Precision.HIGHEST
SMEM = pl.BlockSpec(memory_space=pltpu.SMEM)
VMEM = pl.BlockSpec(memory_space=pltpu.VMEM)
ANY = pl.BlockSpec(memory_space=pl.ANY)
ROOMY = pltpu.CompilerParams(vmem_limit_bytes=60 * 2**20)
CELL_BLOCKS = 64


def bit_orders(nx, ny, far_first=False):
    low = (ny - 1).bit_length()
    near, far = list(range(low)), list(range(low, low + (nx - 1).bit_length()))
    swapped = list(near)
    if low >= 3:
        swapped[1], swapped[2] = swapped[2], swapped[1]
    if far_first:
        return [o[:1] + far + o[1:] for o in (near, swapped)]
    return [o + far for o in (near, swapped)]


def place_in(order, owner):
    place = 0
    for bit in order:
        place = place * 2 + ((owner >> bit) & 1)
    return place


def pair_table(owned):
    if owned % 8:
        return [(0, owned // 2, False)]
    return [(0, owned // 4, False), (owned // 2, owned // 8, True), (3 * owned // 4, owned // 8, False)]


def list_tiles(nx, ny, pairs, owned, rows, cols, live, order, slots, list_row, list_tile, list_slot):
    devices = nx * ny
    me = lax.axis_index("gx") * ny + lax.axis_index("gy")

    @pl.loop(0, slots.shape[0])
    def _(b):
        slots[b] = -1

    total = 0
    for first, each, far_first in pairs:
        size = devices * each // 2
        for part, bits in enumerate(bit_orders(nx, ny, far_first)):
            mine = place_in(bits, me)
            for owner in range(devices):
                place = (place_in(bits, owner) ^ mine) * each
                place += jnp.where(place < size, 0, size) + part * size + total
                for j in range(each):
                    slots[order[owner * owned + first + part * each + j]] = place + j
        total += 4 * size

    room = list_tile.shape[0] // len(pairs)
    ends = [sum(2 * e * devices for _, e, _ in pairs[: k + 1]) for k in range(len(pairs))]

    def step(t, found):
        slot = slots[cols[t]]
        row = rows[t]
        later = []
        for k in range(len(pairs)):
            at = found[k] + k * room
            list_tile[at] = t
            list_row[at] = row
            list_slot[at] = slot
            low = ends[k - 1] if k else 0
            later.append(found[k] + jnp.logical_and(slot >= low, slot < ends[k]).astype(jnp.int32))
        return tuple(later)

    found = lax.fori_loop(0, live, step, (jnp.int32(0),) * len(pairs))
    for k in range(len(pairs)):
        for u in range(GROUP):
            list_tile[found[k] + k * room + u] = 0
            list_row[found[k] + k * room + u] = 0
            list_slot[found[k] + k * room + u] = total
    return found


def add_products(found, first, list_row, list_tile, list_slot, tiles_v, split_v, sums_v):
    @pl.loop(0, (found + GROUP - 1) // GROUP)
    def _(q):
        products = []
        for u in range(GROUP):
            k = first + q * GROUP + u
            product = lax.dot_general(
                tiles_v[list_tile[k]],
                split_v[list_row[k]],
                (((0,), (0,)), ((), ())),
                preferred_element_type=jnp.float32,
            )
            n = product.shape[-1] // 2
            products.append(product[:, :n] + product[:, n:])
        for u in range(GROUP):
            sums_v[list_slot[first + q * GROUP + u]] += products[u]


def zero(ref):
    @pl.loop(0, ref.shape[0])
    def _(b):
        ref[b] = jnp.zeros(ref.shape[1:], ref.dtype)


def add_and_save(pairs, found, list_row, list_tile, list_slot, tiles_v, split_v, sums_v, pieces, sem):
    saves = []
    base = 0
    room = list_tile.shape[0] // len(pairs)
    for p in range(len(pairs)):
        add_products(found[p], p * room, list_row, list_tile, list_slot, tiles_v, split_v, sums_v)
        size = pieces[8 * p].shape[0]
        for k in (5, 7, 4, 6, 1, 3, 0, 2):
            at = pl.ds(base + k * size, size)
            to = pieces[8 * p + k].at[pl.ds(0, size)]
            saves.append(pltpu.make_async_copy(sums_v.at[at], to, sem.at[8 * p + k]))
            saves[-1].start()
        base += 8 * size
    for s in saves:
        s.wait()


def first_kernel(nx, ny, pairs, owned, rows, cols, count, order, tiles, sketch, *refs):
    n_pieces = 8 * len(pairs)
    pieces, split_out = refs[:n_pieces], refs[n_pieces]
    (
        sketch_v, tiles_v, y_v, split_v, sums_v, gram_v, slots, list_row, list_tile, list_slot,
        sem_s, sem_t, sem_y, sem_p, sem_g,
    ) = refs[n_pieces + 1 :]
    cell_blocks = split_v.shape[0]
    live = count[0]
    groups = (live + GROUP - 1) // GROUP

    def load_tiles(g):
        at = pl.ds(g * GROUP, GROUP)
        return pltpu.make_async_copy(tiles.at[at], tiles_v.at[at], sem_t.at[g])

    @pl.loop(0, groups)
    def _(g):
        load_tiles(g).start()
        for u in range(GROUP):
            t = g * GROUP + u
            pltpu.make_async_copy(sketch.at[cols[t]], sketch_v.at[t], sem_s.at[g]).start()

    zero(y_v)
    zero(sums_v)
    found = list_tiles(nx, ny, pairs, owned, rows, cols, live, order, slots, list_row, list_tile, list_slot)

    @pl.loop(0, groups)
    def _(g):
        load_tiles(g).wait()
        at = pl.ds(g * GROUP, GROUP)
        pltpu.make_async_copy(sketch.at[pl.ds(0, GROUP)], sketch_v.at[at], sem_s.at[g]).wait()
        products = []
        for u in range(GROUP):
            t = g * GROUP + u
            products.append(jnp.dot(tiles_v[t], sketch_v[t], preferred_element_type=jnp.float32))
        for u in range(GROUP):
            t = g * GROUP + u
            y_v[jnp.where(t < live, rows[t], cell_blocks)] += products[u]

    gram_v[...] = jnp.zeros_like(gram_v)

    @pl.loop(0, cell_blocks // 8)
    def _(b):
        at = pl.ds(b * 8, 8)
        y = y_v[at]
        high = y.astype(jnp.bfloat16)
        low = (y - high.astype(jnp.float32)).astype(jnp.bfloat16)
        both = jnp.concatenate([high, low], axis=-1)
        split_v[at] = both
        rows = y.shape[0] * y.shape[1]
        gram_v[0] += lax.dot_general(
            high.reshape(rows, -1), both.reshape(rows, -1), (((0,), (0,)), ((), ())), preferred_element_type=jnp.float32
        )

    save_split = pltpu.make_async_copy(split_v, split_out, sem_y)
    save_split.start()
    n = y_v.shape[-1]
    cross = gram_v[0, :, n:]
    gram_v[0, :, :n] += cross + cross.T
    rider = pieces[-3]
    save_gram = pltpu.make_async_copy(gram_v.at[:, :, pl.ds(0, n)], rider.at[pl.ds(rider.shape[0] - 1, 1)], sem_g)
    save_gram.start()
    add_and_save(pairs, found, list_row, list_tile, list_slot, tiles_v, split_v, sums_v, pieces, sem_p)
    save_split.wait()
    save_gram.wait()


def second_kernel(nx, ny, pairs, owned, rows, cols, count, order, tiles, split, *refs):
    pieces = refs[: 8 * len(pairs)]
    tiles_v, split_v, sums_v, slots, list_row, list_tile, list_slot, sem_t, sem_y, sem_p = refs[8 * len(pairs) :]
    live = count[0]
    load_split = pltpu.make_async_copy(split, split_v, sem_y)
    load_tiles = pltpu.make_async_copy(tiles, tiles_v, sem_t)
    load_split.start()
    load_tiles.start()
    zero(sums_v)
    found = list_tiles(nx, ny, pairs, owned, rows, cols, live, order, slots, list_row, list_tile, list_slot)
    load_split.wait()
    load_tiles.wait()
    add_and_save(pairs, found, list_row, list_tile, list_slot, tiles_v, split_v, sums_v, pieces, sem_p)


def combine_kernel(counts, *refs):
    out = refs[-1]
    first = row = 0
    for terms, size in counts:
        total = refs[first][...]
        for k in range(1, terms):
            total += refs[first + k][...]
        out[pl.ds(row, size)] = total
        first += terms
        row += size


def inverse_factor(gram, beside=lambda panel: None):
    n = gram.shape[0]
    row = lax.broadcasted_iota(jnp.int32, (PANEL, n), 0)
    eye = lax.broadcasted_iota(jnp.int32, (n, n), 0) == lax.broadcasted_iota(jnp.int32, (n, n), 1)
    rest = jnp.concatenate([gram, eye.astype(jnp.float32)], axis=1)
    done = []
    for p in range(0, n, PANEL):
        a, w = rest[:PANEL, :n], rest[:PANEL, n:]
        columns = [jnp.broadcast_to(a[:, p + t : p + t + 1], (PANEL, n)) for t in range(PANEL)]
        scale = jnp.zeros((PANEL, n), jnp.float32)
        for s in range(PANEL):
            pivot = columns[s][s : s + 1]
            scale = jnp.where(row == s, lax.rsqrt(pivot), scale)
            if s + 1 < PANEL:
                factor = jnp.where(row > s, columns[s] * (1.0 / pivot), 0.0)
                for t in range(s + 1, PANEL):
                    columns[t] = columns[t] - factor * columns[t][s : s + 1]
                a = a - factor * a[s : s + 1]
                w = w - factor * w[s : s + 1]
        a, w = a * scale, w * scale
        done.append(w)
        beside(p // PANEL)
        if p + PANEL < n:
            update = lax.dot_general(
                a, jnp.concatenate([a, w], axis=1), (((0,), (0,)), ((), ())),
                precision=EXACT, preferred_element_type=jnp.float32,
            )
            rest = rest[PANEL:] - update[p + PANEL :]
    return jnp.concatenate(done, axis=0)


def times_transposed(x, w):
    return lax.dot_general(x, w, (((1,), (1,)), ((), ())), precision=EXACT, preferred_element_type=jnp.float32)


def total_of(refs):
    return functools.reduce(jnp.add, [r[...].reshape(r.shape[-2:]) for r in refs])


def factor_kernel(scale, *refs):
    gram, out = refs[:-1], refs[-1]
    out[...] = (inverse_factor(total_of(gram)) * scale).T


def owned_kernel(counts, has_gram, inverse, *refs):
    gram, terms, (z_out, gram_out) = refs[:has_gram], refs[has_gram:-2], refs[-2:]
    rows = []
    first = 0
    for k in counts:
        rows.append(functools.reduce(jnp.add, [t[...] for t in terms[first : first + k]]))
        first += k
    raw = jnp.concatenate(rows, axis=0) if len(rows) > 1 else rows[0]
    raw = raw.reshape(-1, raw.shape[-1])
    z = jnp.dot(raw, inverse[...], precision=EXACT, preferred_element_type=jnp.float32)
    z_out[...] = z
    g = lax.dot_general(z, z, (((0,), (0,)), ((), ())), precision=EXACT, preferred_element_type=jnp.float32)
    if has_gram:
        g += gram[0][0]
    gram_out[0] = g


def last_kernel(scale, n_grams, split, inverse, *refs):
    split_v, out_v, sem_in, sem_out = refs[-4:]
    grams, zs = refs[:n_grams], refs[n_grams:-6]
    out, cells = refs[-6:-4]
    chunks = sem_in.shape[0]
    blocks, side, both = split_v.shape
    chunk, n = blocks // chunks, both // 2
    rows = chunk * side
    loads, saves = [], []
    for c in range(chunks):
        at = pl.ds(c * chunk, chunk)
        loads.append(pltpu.make_async_copy(split.at[at], split_v.at[at], sem_in.at[c]))
        at = pl.ds(c * rows, rows)
        saves.append(pltpu.make_async_copy(out_v.at[at], cells.at[at], sem_out.at[c]))
        loads[c].start()
    high = inverse[...].astype(jnp.bfloat16)
    low = (inverse[...] - high.astype(jnp.float32)).astype(jnp.bfloat16)
    right = jnp.concatenate(
        [jnp.concatenate([high, low], axis=1), jnp.concatenate([high, jnp.zeros_like(low)], axis=1)], axis=0
    )

    def cell_rows(c):
        loads[c].wait()
        y = split_v[pl.ds(c * chunk, chunk)].reshape(rows, both)
        g = jnp.dot(y, right, preferred_element_type=jnp.float32)
        out_v[pl.ds(c * rows, rows), :] = (g[:, :n] + g[:, n:]).astype(out_v.dtype)
        saves[c].start()

    w = inverse_factor(total_of(grams), cell_rows) * scale
    at = 0
    for z in zs:
        out[pl.ds(at, z.shape[0]), :] = times_transposed(z[...], w)
        at += z.shape[0]
    for save in saves:
        save.wait()


def cost(microseconds):
    return pl.CostEstimate(flops=int(microseconds * 1e9), bytes_accessed=int(microseconds * 3e6), transcendentals=0)


def on_device(tiles, tile_rows, tile_cols, tile_counts, block_order, sketch, nx, ny):
    slots_all, side, _ = tiles.shape
    genes, wide = sketch.shape
    blocks = genes // side
    devices = nx * ny
    owned = blocks // devices
    table = pair_table(owned)
    orders = bit_orders(nx, ny)
    early_pairs, late_pairs = table[:2], table[2:]
    f32, bf16 = jnp.float32, jnp.bfloat16

    def piece_shapes(pairs, rider):
        sizes = [devices * each // 4 for _, each, _ in pairs for _ in range(8)]
        sizes[-3] += rider
        return [jax.ShapeDtypeStruct((n, side, wide), f32) for n in sizes]

    def list_scratch(pairs):
        room = slots_all + GROUP
        return [pltpu.SMEM((blocks,), jnp.int32)] + [pltpu.SMEM((len(pairs) * room,), jnp.int32)] * 3

    def sums_scratch(pairs):
        return pltpu.VMEM((sum(2 * each for _, each, _ in pairs) * devices + 1, side, wide), f32)

    def swap(value, bit):
        partner = 1 << bit
        if partner < ny:
            return lax.ppermute(value, "gy", [(i, i ^ partner) for i in range(ny)])
        partner //= ny
        return lax.ppermute(value, "gx", [(i, i ^ partner) for i in range(nx)])

    *early, split = pl.pallas_call(
        functools.partial(first_kernel, nx, ny, early_pairs, owned),
        out_shape=piece_shapes(early_pairs, 1)
        + [jax.ShapeDtypeStruct((CELL_BLOCKS, side, 2 * wide), bf16)],
        in_specs=[SMEM] * 4 + [ANY] * 2,
        out_specs=[ANY] * (8 * len(early_pairs) + 1),
        scratch_shapes=[
            pltpu.VMEM((slots_all, side, wide), bf16),
            pltpu.VMEM((slots_all, side, side), bf16),
            pltpu.VMEM((CELL_BLOCKS + 1, side, wide), f32),
            pltpu.VMEM((CELL_BLOCKS, side, 2 * wide), bf16),
            sums_scratch(early_pairs),
            pltpu.VMEM((1, wide, 2 * wide), f32),
            *list_scratch(early_pairs),
            pltpu.SemaphoreType.DMA((slots_all // GROUP,)),
            pltpu.SemaphoreType.DMA((slots_all // GROUP,)),
            pltpu.SemaphoreType.DMA,
            pltpu.SemaphoreType.DMA((8 * len(early_pairs),)),
            pltpu.SemaphoreType.DMA,
        ],
        compiler_params=ROOMY,
        cost_estimate=cost(4.0),
        name="tile_products",
    )(tile_rows, tile_cols, tile_counts, block_order, tiles, sketch.reshape(blocks, side, wide))

    done_before = [tile_counts]

    def follows(value):
        return lax.optimization_barrier((value, done_before[0]))[0]

    def note(value):
        done_before[0] = value
        return value

    bits = orders[0]
    shared = next(k for k in range(1, len(bits)) if all(o[k:] == bits[k:] for o in orders))
    orders_of = [bit_orders(nx, ny, far_first) for _, _, far_first in table]
    state = {}

    def begin(pair, *arrays):
        kept, quarters = arrays[:4], arrays[4:]
        half = kept[0].shape[0]
        terms = [[[(kept[2 * part + upper], 0)] for upper in range(2)] for part in range(2)]
        state[pair] = [1, half, terms, []]
        if quarters[1].shape[0] > half:
            state[pair][3] = [(quarters[1], half)]

        for k in (1, 3, 0, 2):
            got = swap(quarters[k], orders_of[pair][0][0])
            terms[k // 2][k % 2].append((got, 0))
            if k == 1 and state[pair][3]:
                state[pair][3].append((got, half))

    def wait(pairs):
        found = []
        for pair in pairs:
            _, _, terms, rider = state[pair]
            for array, _ in [terms[part][1][-1] for part in range(2)] + rider[-1:]:
                if not any(array is f for f in found):
                    found.append(array)
        ready = lax.optimization_barrier((*found, done_before[0]))

        def swapped(term):
            return next(((r, term[1]) for f, r in zip(found, ready) if f is term[0]), term)

        for pair in pairs:
            step, size, terms, rider = state[pair]
            terms = [[[swapped(t) for t in upper] for upper in part] for part in terms]
            state[pair] = [step, size, terms, [swapped(t) for t in rider]]

    def combine(groups):
        counts = tuple((len(terms), size) for terms, size in groups)
        specs, arrays = [], []
        for terms, size in groups:
            for array, at in terms:
                specs.append(pl.BlockSpec((size, side, wide), functools.partial(lambda place, _: (place, 0, 0), at // size)))
                arrays.append(array)
        rows = sum(size for _, size in groups)
        return pl.pallas_call(
            functools.partial(combine_kernel, counts),
            grid=(1,),
            out_shape=jax.ShapeDtypeStruct((rows, side, wide), f32),
            in_specs=specs,
            out_specs=pl.BlockSpec((rows, side, wide), lambda _: (0, 0, 0)),
            compiler_params=pltpu.CompilerParams(vmem_limit_bytes=24 * 2**20),
            cost_estimate=cost(0.01),
            name="combine",
        )(*arrays)

    def halves(size, base, got):
        cut = size // 2
        return [[(array, at + upper * cut) for array, at in (base, got)] for upper in range(2)]

    def send_apart(pair, carrier=0):
        step, size, terms, rider = state[pair]
        sent, got = [], []
        for part in range(2):
            groups = [(terms[part][1], size)] + ([(rider, 1)] if rider and part == carrier else [])
            sent.append(note(combine(groups)))
            got.append(swap(sent[part], orders_of[pair][part][step]))
        base = [combine([(terms[part][0], size)]) for part in range(2)]
        rider = [(sent[carrier], size), (got[carrier], size)] if rider else []
        state[pair] = [step + 1, size // 2, [halves(size, (base[part], 0), (got[part], 0)) for part in range(2)], rider]

    def hand_over(pair, other):
        state[other][3], state[pair][3] = state[pair][3], []

    def send_both_upper(pair):
        step, size, terms, rider = state[pair]
        sent = note(combine([(terms[part][1], size) for part in range(2)] + ([(rider, 1)] if rider else [])))
        return sent, swap(sent, orders_of[pair][0][step])

    def keep_both_lower(pair, sent, got):
        step, size, terms, rider = state[pair]
        base = combine([(terms[part][0], size) for part in range(2)])
        rider = [(sent, 2 * size), (got, 2 * size)] if rider else []
        state[pair] = [step + 1, size // 2, [halves(size, (base, part * size), (got, part * size)) for part in range(2)], rider]

    def send_both(pair):
        keep_both_lower(pair, *send_both_upper(pair))

    def term_specs(groups):
        specs, arrays = [], []
        for terms, size in groups:
            for array, at in terms:
                specs.append(pl.BlockSpec((size, side, wide), functools.partial(lambda place, _: (place, 0, 0), at // size)))
                arrays.append(array)
        return specs, arrays

    def owners(pairs, inverse, gram=()):
        groups = [(state[p][2][part][0], max(1, 2 * state[p][1])) for p in pairs for part in range(2)]
        specs, arrays = term_specs(groups)
        rows = sum(size for _, size in groups) * side
        whole = pl.BlockSpec((wide, wide), lambda _: (0, 0))
        square = pl.BlockSpec((1, wide, wide), lambda _: (0, 0, 0))
        z, gram = pl.pallas_call(
            functools.partial(owned_kernel, [len(terms) for terms, _ in groups], len(gram)),
            grid=(1,),
            out_shape=[jax.ShapeDtypeStruct((rows, wide), f32), jax.ShapeDtypeStruct((1, wide, wide), f32)],
            in_specs=[whole] + [square] * len(gram) + specs,
            out_specs=[pl.BlockSpec((rows, wide), lambda _: (0, 0)), square],
            compiler_params=pltpu.CompilerParams(vmem_limit_bytes=24 * 2**20),
            cost_estimate=cost(0.5),
            name="owned_gram",
        )(inverse, *gram, *arrays)
        return z, note(gram)

    cells_all = CELL_BLOCKS * side * devices

    def late_products(pairs):
        return pl.pallas_call(
            functools.partial(second_kernel, nx, ny, pairs, owned),
            out_shape=piece_shapes(pairs, 0),
            in_specs=[SMEM] * 4 + [ANY] * 2,
            out_specs=[ANY] * (8 * len(pairs)),
            scratch_shapes=[
                pltpu.VMEM((slots_all, side, side), bf16),
                pltpu.VMEM((CELL_BLOCKS, side, 2 * wide), bf16),
                sums_scratch(pairs),
                *list_scratch(pairs),
                pltpu.SemaphoreType.DMA,
                pltpu.SemaphoreType.DMA,
                pltpu.SemaphoreType.DMA((8 * len(pairs),)),
            ],
            compiler_params=pltpu.CompilerParams(vmem_limit_bytes=36 * 2**20),
            cost_estimate=cost(4.0),
            name="late_products",
        )(tile_rows, tile_cols, tile_counts, block_order, tiles, follows(split))

    def cell_inverse(pair):
        specs, arrays = term_specs([(state[pair][3], 1)])
        return note(
            pl.pallas_call(
                functools.partial(factor_kernel, math.sqrt(cells_all)),
                grid=(1,),
                out_shape=jax.ShapeDtypeStruct((wide, wide), f32),
                in_specs=specs,
                out_specs=pl.BlockSpec((wide, wide), lambda _: (0, 0)),
                cost_estimate=cost(1.5),
                name="cell_cholesky",
            )(follows(arrays[0]), *arrays[1:])
        )

    begin(0, *early[:8])
    if len(table) == 1:
        for step in range(1, len(bits)):
            wait([0])
            send_apart(0) if step < shared else send_both(0)
        wait([0])
        inverse = cell_inverse(0)
        zs, gene_gram = [None], None
        zs[0], gene_gram = owners([0], inverse)
    else:
        begin(1, *early[8:])
        wait([0])
        send_apart(0)
        wait([1])
        send_both(1)
        late = late_products(late_pairs)
        note(late[0])
        begin(2, *late)
        wait([0])
        send_apart(0)
        wait([1])
        send_both(1)
        wait([2])
        send_apart(2)
        wait([0, 1, 2])
        hand_over(1, 2)
        send_both(0)
        send_apart(2)
        send_apart(1)
        wait([0, 1, 2])
        hand_over(2, 1)
        send_both(0)
        send_both(2)
        send_apart(1, 1)
        wait([0, 1, 2])
        send_both(2)
        inverse = cell_inverse(1)
        z_early, gene_gram = owners([0, 1], inverse)
        wait([2])
        z_late, gene_gram = owners([2], inverse, (gene_gram,))
        zs = [z_early, z_late]

    grams = [gene_gram]
    for k, bit in enumerate(bits):
        if k:
            grams = [combine([([(g, 0) for g in grams], 1)])]
        grams.append(swap(grams[0], bit))
    chunks = wide // PANEL
    gene_factor, cell_factor = pl.pallas_call(
        functools.partial(last_kernel, math.sqrt(genes), len(grams)),
        out_shape=[
            jax.ShapeDtypeStruct((owned * side, wide), f32),
            jax.ShapeDtypeStruct((CELL_BLOCKS * side, wide), bf16),
        ],
        in_specs=[ANY] + [VMEM] * (1 + len(grams) + len(zs)),
        out_specs=[VMEM, ANY],
        scratch_shapes=[
            pltpu.VMEM((CELL_BLOCKS, side, 2 * wide), bf16),
            pltpu.VMEM((CELL_BLOCKS * side, wide), bf16),
            pltpu.SemaphoreType.DMA((chunks,)),
            pltpu.SemaphoreType.DMA((chunks,)),
        ],
        compiler_params=pltpu.CompilerParams(vmem_limit_bytes=20 * 2**20),
        name="factors",
    )(split, inverse, *grams, *zs)
    return (cell_factor, gene_factor)


def solution(mesh):
    placed = (
        P(("gx", "gy"), None, None),
        P(("gx", "gy")),
        P(("gx", "gy")),
        P(("gx", "gy")),
        P(),
        P(),
    )
    return jax.shard_map(
        functools.partial(on_device, nx=mesh.shape["gx"], ny=mesh.shape["gy"]),
        mesh=mesh,
        in_specs=placed,
        out_specs=(P(("gx", "gy"), None), P(("gx", "gy"), None)),
        check_vma=False,
    )
```

```python
import functools
import math

import jax
import jax.numpy as jnp
from jax import lax
from jax.experimental import pallas as pl
from jax.experimental.pallas import tpu as pltpu
from jax.sharding import PartitionSpec as P

GROUP = 16
PANEL = 32
EXACT = lax.Precision.HIGHEST
SMEM = pl.BlockSpec(memory_space=pltpu.SMEM)
VMEM = pl.BlockSpec(memory_space=pltpu.VMEM)
ANY = pl.BlockSpec(memory_space=pl.ANY)
ROOMY = pltpu.CompilerParams(vmem_limit_bytes=60 * 2**20)
CELL_BLOCKS = 64


def bit_orders(nx, ny, far_first=False):
    low = (ny - 1).bit_length()
    near, far = list(range(low)), list(range(low, low + (nx - 1).bit_length()))
    swapped = list(near)
    if low >= 3:
        swapped[1], swapped[2] = swapped[2], swapped[1]
    if far_first:
        return [o[:1] + far + o[1:] for o in (near, swapped)]
    return [o + far for o in (near, swapped)]


def place_in(order, owner):
    place = 0
    for bit in order:
        place = place * 2 + ((owner >> bit) & 1)
    return place


def pair_table(owned):
    if owned % 8:
        return [(0, owned // 2, False)]
    return [(0, owned // 4, False), (owned // 2, owned // 8, True), (3 * owned // 4, owned // 8, False)]


def list_tiles(nx, ny, pairs, owned, rows, cols, live, order, slots, list_row, list_tile, list_slot):
    devices = nx * ny
    me = lax.axis_index("gx") * ny + lax.axis_index("gy")

    @pl.loop(0, slots.shape[0] // 16)
    def _(b):
        for j in range(16):
            slots[b * 16 + j] = -1

    total = 0
    for first, each, far_first in pairs:
        size = devices * each // 2
        for part, bits in enumerate(bit_orders(nx, ny, far_first)):
            mine = place_in(bits, me)
            for owner in range(devices):
                place = (place_in(bits, owner) ^ mine) * each
                place += jnp.where(place < size, 0, size) + part * size + total
                for j in range(each):
                    slots[order[owner * owned + first + part * each + j]] = place + j
        total += 4 * size

    room = list_tile.shape[0] // len(pairs)
    ends = [sum(2 * e * devices for _, e, _ in pairs[: k + 1]) for k in range(len(pairs))]

    def step(t, found):
        slot = slots[cols[t]]
        row = rows[t]
        later = []
        for k in range(len(pairs)):
            at = found[k] + k * room
            list_tile[at] = t
            list_row[at] = row
            list_slot[at] = slot
            low = ends[k - 1] if k else 0
            later.append(found[k] + jnp.logical_and(slot >= low, slot < ends[k]).astype(jnp.int32))
        return tuple(later)

    found = lax.fori_loop(0, live, step, (jnp.int32(0),) * len(pairs))
    for k in range(len(pairs)):
        for u in range(GROUP):
            list_tile[found[k] + k * room + u] = 0
            list_row[found[k] + k * room + u] = 0
            list_slot[found[k] + k * room + u] = total
    return found


def add_products(found, first, list_row, list_tile, list_slot, tiles_v, split_v, sums_v):
    @pl.loop(0, (found + GROUP - 1) // GROUP)
    def _(q):
        products = []
        for u in range(GROUP):
            k = first + q * GROUP + u
            product = lax.dot_general(
                tiles_v[list_tile[k]],
                split_v[list_row[k]],
                (((0,), (0,)), ((), ())),
                preferred_element_type=jnp.float32,
            )
            n = product.shape[-1] // 2
            products.append(product[:, :n] + product[:, n:])
        for u in range(GROUP):
            sums_v[list_slot[first + q * GROUP + u]] += products[u]


def zero(ref):
    @pl.loop(0, ref.shape[0])
    def _(b):
        ref[b] = jnp.zeros(ref.shape[1:], ref.dtype)


def add_and_save(pairs, found, list_row, list_tile, list_slot, tiles_v, split_v, sums_v, pieces, sem):
    saves = []
    base = 0
    room = list_tile.shape[0] // len(pairs)
    for p in range(len(pairs)):
        add_products(found[p], p * room, list_row, list_tile, list_slot, tiles_v, split_v, sums_v)
        size = pieces[8 * p].shape[0]
        for k in (5, 7, 4, 6, 1, 3, 0, 2):
            at = pl.ds(base + k * size, size)
            to = pieces[8 * p + k].at[pl.ds(0, size)]
            saves.append(pltpu.make_async_copy(sums_v.at[at], to, sem.at[8 * p + k]))
            saves[-1].start()
        base += 8 * size
    for s in saves:
        s.wait()


def first_kernel(nx, ny, pairs, owned, rows, cols, count, order, tiles, sketch, *refs):
    n_pieces = 8 * len(pairs)
    pieces, split_out = refs[:n_pieces], refs[n_pieces]
    (
        sketch_v, tiles_v, y_v, split_v, sums_v, gram_v, slots, list_row, list_tile, list_slot,
        sem_s, sem_t, sem_y, sem_p, sem_g,
    ) = refs[n_pieces + 1 :]
    cell_blocks = split_v.shape[0]
    live = count[0]
    groups = (live + GROUP - 1) // GROUP

    def load_tiles(g):
        at = pl.ds(g * GROUP, GROUP)
        return pltpu.make_async_copy(tiles.at[at], tiles_v.at[at], sem_t.at[g])

    @pl.loop(0, groups)
    def _(g):
        load_tiles(g).start()
        for u in range(GROUP):
            t = g * GROUP + u
            pltpu.make_async_copy(sketch.at[cols[t]], sketch_v.at[t], sem_s.at[g]).start()

    zero(y_v)
    found = list_tiles(nx, ny, pairs, owned, rows, cols, live, order, slots, list_row, list_tile, list_slot)

    @pl.loop(0, groups)
    def _(g):
        load_tiles(g).wait()
        at = pl.ds(g * GROUP, GROUP)
        pltpu.make_async_copy(sketch.at[pl.ds(0, GROUP)], sketch_v.at[at], sem_s.at[g]).wait()
        products = []
        for u in range(GROUP):
            t = g * GROUP + u
            products.append(jnp.dot(tiles_v[t], sketch_v[t], preferred_element_type=jnp.float32))
        for u in range(GROUP):
            t = g * GROUP + u
            y_v[jnp.where(t < live, rows[t], cell_blocks)] += products[u]

    gram_v[...] = jnp.zeros_like(gram_v)

    turns = cell_blocks // 8
    share = sums_v.shape[0] // turns

    @pl.loop(0, turns)
    def _(b):
        for j in range(share):
            sums_v[b * share + j] = jnp.zeros(sums_v.shape[1:], sums_v.dtype)
        at = pl.ds(b * 8, 8)
        y = y_v[at]
        high = y.astype(jnp.bfloat16)
        low = (y - high.astype(jnp.float32)).astype(jnp.bfloat16)
        both = jnp.concatenate([high, low], axis=-1)
        split_v[at] = both
        rows = y.shape[0] * y.shape[1]
        gram_v[0] += lax.dot_general(
            high.reshape(rows, -1), both.reshape(rows, -1), (((0,), (0,)), ((), ())), preferred_element_type=jnp.float32
        )

    save_split = pltpu.make_async_copy(split_v, split_out, sem_y)
    save_split.start()
    n = y_v.shape[-1]
    cross = gram_v[0, :, n:]
    gram_v[0, :, :n] += cross + cross.T
    rider = pieces[-3]
    save_gram = pltpu.make_async_copy(gram_v.at[:, :, pl.ds(0, n)], rider.at[pl.ds(rider.shape[0] - 1, 1)], sem_g)
    save_gram.start()
    add_and_save(pairs, found, list_row, list_tile, list_slot, tiles_v, split_v, sums_v, pieces, sem_p)
    save_split.wait()
    save_gram.wait()


def second_kernel(nx, ny, pairs, owned, rows, cols, count, order, tiles, split, *refs):
    pieces = refs[: 8 * len(pairs)]
    tiles_v, split_v, sums_v, slots, list_row, list_tile, list_slot, sem_t, sem_y, sem_p = refs[8 * len(pairs) :]
    live = count[0]
    load_split = pltpu.make_async_copy(split, split_v, sem_y)
    load_tiles = pltpu.make_async_copy(tiles, tiles_v, sem_t)
    load_split.start()
    load_tiles.start()
    zero(sums_v)
    found = list_tiles(nx, ny, pairs, owned, rows, cols, live, order, slots, list_row, list_tile, list_slot)
    load_split.wait()
    load_tiles.wait()
    add_and_save(pairs, found, list_row, list_tile, list_slot, tiles_v, split_v, sums_v, pieces, sem_p)


def combine_kernel(counts, *refs):
    out = refs[-1]
    first = row = 0
    for terms, size in counts:
        total = refs[first][...]
        for k in range(1, terms):
            total += refs[first + k][...]
        out[pl.ds(row, size)] = total
        first += terms
        row += size


def inverse_factor(gram, beside=lambda panel: None):
    n = gram.shape[0]
    row = lax.broadcasted_iota(jnp.int32, (PANEL, n), 0)
    eye = lax.broadcasted_iota(jnp.int32, (n, n), 0) == lax.broadcasted_iota(jnp.int32, (n, n), 1)
    rest = jnp.concatenate([gram, eye.astype(jnp.float32)], axis=1)
    done = []
    for p in range(0, n, PANEL):
        a, w = rest[:PANEL, :n], rest[:PANEL, n:]
        columns = [jnp.broadcast_to(a[:, p + t : p + t + 1], (PANEL, n)) for t in range(PANEL)]
        scale = jnp.zeros((PANEL, n), jnp.float32)
        for s in range(PANEL):
            pivot = columns[s][s : s + 1]
            scale = jnp.where(row == s, lax.rsqrt(pivot), scale)
            if s + 1 < PANEL:
                factor = jnp.where(row > s, columns[s] * (1.0 / pivot), 0.0)
                for t in range(s + 1, PANEL):
                    columns[t] = columns[t] - factor * columns[t][s : s + 1]
                a = a - factor * a[s : s + 1]
                w = w - factor * w[s : s + 1]
        a, w = a * scale, w * scale
        done.append(w)
        beside(p // PANEL)
        if p + PANEL < n:
            update = lax.dot_general(
                a, jnp.concatenate([a, w], axis=1), (((0,), (0,)), ((), ())),
                precision=EXACT, preferred_element_type=jnp.float32,
            )
            rest = rest[PANEL:] - update[p + PANEL :]
    return jnp.concatenate(done, axis=0)


def times_transposed(x, w):
    return lax.dot_general(x, w, (((1,), (1,)), ((), ())), precision=EXACT, preferred_element_type=jnp.float32)


def total_of(refs):
    return functools.reduce(jnp.add, [r[...].reshape(r.shape[-2:]) for r in refs])


def factor_kernel(scale, *refs):
    gram, out = refs[:-1], refs[-1]
    out[...] = (inverse_factor(total_of(gram)) * scale).T


def owned_kernel(counts, has_gram, inverse, *refs):
    gram, terms, (z_out, gram_out) = refs[:has_gram], refs[has_gram:-2], refs[-2:]
    rows = []
    first = 0
    for k in counts:
        rows.append(functools.reduce(jnp.add, [t[...] for t in terms[first : first + k]]))
        first += k
    raw = jnp.concatenate(rows, axis=0) if len(rows) > 1 else rows[0]
    raw = raw.reshape(-1, raw.shape[-1])
    z = jnp.dot(raw, inverse[...], precision=EXACT, preferred_element_type=jnp.float32)
    z_out[...] = z
    g = lax.dot_general(z, z, (((0,), (0,)), ((), ())), precision=EXACT, preferred_element_type=jnp.float32)
    if has_gram:
        g += gram[0][0]
    gram_out[0] = g


def last_kernel(scale, n_grams, split, inverse, *refs):
    split_v, out_v, sem_in, sem_out = refs[-4:]
    grams, zs = refs[:n_grams], refs[n_grams:-6]
    out, cells = refs[-6:-4]
    chunks = sem_in.shape[0]
    blocks, side, both = split_v.shape
    chunk, n = blocks // chunks, both // 2
    rows = chunk * side
    loads, saves = [], []
    for c in range(chunks):
        at = pl.ds(c * chunk, chunk)
        loads.append(pltpu.make_async_copy(split.at[at], split_v.at[at], sem_in.at[c]))
        at = pl.ds(c * rows, rows)
        saves.append(pltpu.make_async_copy(out_v.at[at], cells.at[at], sem_out.at[c]))
        loads[c].start()
    high = inverse[...].astype(jnp.bfloat16)
    low = (inverse[...] - high.astype(jnp.float32)).astype(jnp.bfloat16)
    right = jnp.concatenate(
        [jnp.concatenate([high, low], axis=1), jnp.concatenate([high, jnp.zeros_like(low)], axis=1)], axis=0
    )

    def cell_rows(c):
        loads[c].wait()
        y = split_v[pl.ds(c * chunk, chunk)].reshape(rows, both)
        g = jnp.dot(y, right, preferred_element_type=jnp.float32)
        out_v[pl.ds(c * rows, rows), :] = (g[:, :n] + g[:, n:]).astype(out_v.dtype)
        saves[c].start()

    w = inverse_factor(total_of(grams), cell_rows) * scale
    at = 0
    for z in zs:
        out[pl.ds(at, z.shape[0]), :] = times_transposed(z[...], w)
        at += z.shape[0]
    for save in saves:
        save.wait()


def cost(microseconds):
    return pl.CostEstimate(flops=int(microseconds * 1e9), bytes_accessed=int(microseconds * 3e6), transcendentals=0)


def on_device(tiles, tile_rows, tile_cols, tile_counts, block_order, sketch, nx, ny):
    slots_all, side, _ = tiles.shape
    genes, wide = sketch.shape
    blocks = genes // side
    devices = nx * ny
    owned = blocks // devices
    table = pair_table(owned)
    orders = bit_orders(nx, ny)
    early_pairs, late_pairs = table[:2], table[2:]
    f32, bf16 = jnp.float32, jnp.bfloat16

    def piece_shapes(pairs, rider):
        sizes = [devices * each // 4 for _, each, _ in pairs for _ in range(8)]
        sizes[-3] += rider
        return [jax.ShapeDtypeStruct((n, side, wide), f32) for n in sizes]

    def list_scratch(pairs):
        room = slots_all + GROUP
        return [pltpu.SMEM((blocks,), jnp.int32)] + [pltpu.SMEM((len(pairs) * room,), jnp.int32)] * 3

    def sums_scratch(pairs):
        return pltpu.VMEM((sum(2 * each for _, each, _ in pairs) * devices + 8, side, wide), f32)

    def swap(value, bit):
        partner = 1 << bit
        if partner < ny:
            return lax.ppermute(value, "gy", [(i, i ^ partner) for i in range(ny)])
        partner //= ny
        return lax.ppermute(value, "gx", [(i, i ^ partner) for i in range(nx)])

    *early, split = pl.pallas_call(
        functools.partial(first_kernel, nx, ny, early_pairs, owned),
        out_shape=piece_shapes(early_pairs, 1)
        + [jax.ShapeDtypeStruct((CELL_BLOCKS, side, 2 * wide), bf16)],
        in_specs=[SMEM] * 4 + [ANY] * 2,
        out_specs=[ANY] * (8 * len(early_pairs) + 1),
        scratch_shapes=[
            pltpu.VMEM((slots_all, side, wide), bf16),
            pltpu.VMEM((slots_all, side, side), bf16),
            pltpu.VMEM((CELL_BLOCKS + 1, side, wide), f32),
            pltpu.VMEM((CELL_BLOCKS, side, 2 * wide), bf16),
            sums_scratch(early_pairs),
            pltpu.VMEM((1, wide, 2 * wide), f32),
            *list_scratch(early_pairs),
            pltpu.SemaphoreType.DMA((slots_all // GROUP,)),
            pltpu.SemaphoreType.DMA((slots_all // GROUP,)),
            pltpu.SemaphoreType.DMA,
            pltpu.SemaphoreType.DMA((8 * len(early_pairs),)),
            pltpu.SemaphoreType.DMA,
        ],
        compiler_params=ROOMY,
        cost_estimate=cost(4.0),
        name="tile_products",
    )(tile_rows, tile_cols, tile_counts, block_order, tiles, sketch.reshape(blocks, side, wide))

    done_before = [tile_counts]

    def follows(value):
        return lax.optimization_barrier((value, done_before[0]))[0]

    def note(value):
        done_before[0] = value
        return value

    bits = orders[0]
    shared = next(k for k in range(1, len(bits)) if all(o[k:] == bits[k:] for o in orders))
    orders_of = [bit_orders(nx, ny, far_first) for _, _, far_first in table]
    state = {}

    def begin(pair, *arrays):
        kept, quarters = arrays[:4], arrays[4:]
        half = kept[0].shape[0]
        terms = [[[(kept[2 * part + upper], 0)] for upper in range(2)] for part in range(2)]
        state[pair] = [1, half, terms, []]
        if quarters[1].shape[0] > half:
            state[pair][3] = [(quarters[1], half)]

        for k in (1, 3, 0, 2):
            got = swap(quarters[k], orders_of[pair][0][0])
            terms[k // 2][k % 2].append((got, 0))
            if k == 1 and state[pair][3]:
                state[pair][3].append((got, half))

    def wait(pairs):
        found = []
        for pair in pairs:
            _, _, terms, rider = state[pair]
            for array, _ in [terms[part][1][-1] for part in range(2)] + rider[-1:]:
                if not any(array is f for f in found):
                    found.append(array)
        ready = lax.optimization_barrier((*found, done_before[0]))

        def swapped(term):
            return next(((r, term[1]) for f, r in zip(found, ready) if f is term[0]), term)

        for pair in pairs:
            step, size, terms, rider = state[pair]
            terms = [[[swapped(t) for t in upper] for upper in part] for part in terms]
            state[pair] = [step, size, terms, [swapped(t) for t in rider]]

    def combine(groups):
        counts = tuple((len(terms), size) for terms, size in groups)
        specs, arrays = [], []
        for terms, size in groups:
            for array, at in terms:
                specs.append(pl.BlockSpec((size, side, wide), functools.partial(lambda place, _: (place, 0, 0), at // size)))
                arrays.append(array)
        rows = sum(size for _, size in groups)
        return pl.pallas_call(
            functools.partial(combine_kernel, counts),
            grid=(1,),
            out_shape=jax.ShapeDtypeStruct((rows, side, wide), f32),
            in_specs=specs,
            out_specs=pl.BlockSpec((rows, side, wide), lambda _: (0, 0, 0)),
            compiler_params=pltpu.CompilerParams(vmem_limit_bytes=24 * 2**20),
            cost_estimate=cost(0.01),
            name="combine",
        )(*arrays)

    def halves(size, base, got):
        cut = size // 2
        return [[(array, at + upper * cut) for array, at in (base, got)] for upper in range(2)]

    def send_apart(pair, carrier=0):
        step, size, terms, rider = state[pair]
        sent, got = [], []
        for part in range(2):
            groups = [(terms[part][1], size)] + ([(rider, 1)] if rider and part == carrier else [])
            sent.append(note(combine(groups)))
            got.append(swap(sent[part], orders_of[pair][part][step]))
        base = [combine([(terms[part][0], size)]) for part in range(2)]
        rider = [(sent[carrier], size), (got[carrier], size)] if rider else []
        state[pair] = [step + 1, size // 2, [halves(size, (base[part], 0), (got[part], 0)) for part in range(2)], rider]

    def hand_over(pair, other):
        state[other][3], state[pair][3] = state[pair][3], []

    def send_both_upper(pair):
        step, size, terms, rider = state[pair]
        sent = note(combine([(terms[part][1], size) for part in range(2)] + ([(rider, 1)] if rider else [])))
        return sent, swap(sent, orders_of[pair][0][step])

    def keep_both_lower(pair, sent, got):
        step, size, terms, rider = state[pair]
        base = combine([(terms[part][0], size) for part in range(2)])
        rider = [(sent, 2 * size), (got, 2 * size)] if rider else []
        state[pair] = [step + 1, size // 2, [halves(size, (base, part * size), (got, part * size)) for part in range(2)], rider]

    def send_both(pair):
        keep_both_lower(pair, *send_both_upper(pair))

    def term_specs(groups):
        specs, arrays = [], []
        for terms, size in groups:
            for array, at in terms:
                specs.append(pl.BlockSpec((size, side, wide), functools.partial(lambda place, _: (place, 0, 0), at // size)))
                arrays.append(array)
        return specs, arrays

    def owners(pairs, inverse, gram=()):
        groups = [(state[p][2][part][0], max(1, 2 * state[p][1])) for p in pairs for part in range(2)]
        specs, arrays = term_specs(groups)
        rows = sum(size for _, size in groups) * side
        whole = pl.BlockSpec((wide, wide), lambda _: (0, 0))
        square = pl.BlockSpec((1, wide, wide), lambda _: (0, 0, 0))
        z, gram = pl.pallas_call(
            functools.partial(owned_kernel, [len(terms) for terms, _ in groups], len(gram)),
            grid=(1,),
            out_shape=[jax.ShapeDtypeStruct((rows, wide), f32), jax.ShapeDtypeStruct((1, wide, wide), f32)],
            in_specs=[whole] + [square] * len(gram) + specs,
            out_specs=[pl.BlockSpec((rows, wide), lambda _: (0, 0)), square],
            compiler_params=pltpu.CompilerParams(vmem_limit_bytes=24 * 2**20),
            cost_estimate=cost(0.5),
            name="owned_gram",
        )(inverse, *gram, *arrays)
        return z, note(gram)

    cells_all = CELL_BLOCKS * side * devices

    def late_products(pairs):
        return pl.pallas_call(
            functools.partial(second_kernel, nx, ny, pairs, owned),
            out_shape=piece_shapes(pairs, 0),
            in_specs=[SMEM] * 4 + [ANY] * 2,
            out_specs=[ANY] * (8 * len(pairs)),
            scratch_shapes=[
                pltpu.VMEM((slots_all, side, side), bf16),
                pltpu.VMEM((CELL_BLOCKS, side, 2 * wide), bf16),
                sums_scratch(pairs),
                *list_scratch(pairs),
                pltpu.SemaphoreType.DMA,
                pltpu.SemaphoreType.DMA,
                pltpu.SemaphoreType.DMA((8 * len(pairs),)),
            ],
            compiler_params=pltpu.CompilerParams(vmem_limit_bytes=36 * 2**20),
            cost_estimate=cost(4.0),
            name="late_products",
        )(tile_rows, tile_cols, tile_counts, block_order, tiles, follows(split))

    def cell_inverse(pair):
        specs, arrays = term_specs([(state[pair][3], 1)])
        return note(
            pl.pallas_call(
                functools.partial(factor_kernel, math.sqrt(cells_all)),
                grid=(1,),
                out_shape=jax.ShapeDtypeStruct((wide, wide), f32),
                in_specs=specs,
                out_specs=pl.BlockSpec((wide, wide), lambda _: (0, 0)),
                cost_estimate=cost(1.5),
                name="cell_cholesky",
            )(follows(arrays[0]), *arrays[1:])
        )

    begin(0, *early[:8])
    if len(table) == 1:
        for step in range(1, len(bits)):
            wait([0])
            send_apart(0) if step < shared else send_both(0)
        wait([0])
        inverse = cell_inverse(0)
        zs, gene_gram = [None], None
        zs[0], gene_gram = owners([0], inverse)
    else:
        begin(1, *early[8:])
        wait([0])
        send_apart(0)
        wait([1])
        send_both(1)
        late = late_products(late_pairs)
        note(late[0])
        begin(2, *late)
        wait([0])
        send_apart(0)
        wait([1])
        send_both(1)
        wait([2])
        send_apart(2)
        wait([0, 1, 2])
        hand_over(1, 2)
        send_both(0)
        send_apart(2)
        send_apart(1)
        wait([0, 1, 2])
        hand_over(2, 1)
        send_both(0)
        send_both(2)
        send_apart(1, 1)
        wait([0, 1, 2])
        send_both(2)
        inverse = cell_inverse(1)
        z_early, gene_gram = owners([0, 1], inverse)
        wait([2])
        z_late, gene_gram = owners([2], inverse, (gene_gram,))
        zs = [z_early, z_late]

    grams = [gene_gram]
    for k, bit in enumerate(bits):
        if k:
            grams = [combine([([(g, 0) for g in grams], 1)])]
        grams.append(swap(grams[0], bit))
    chunks = wide // PANEL
    gene_factor, cell_factor = pl.pallas_call(
        functools.partial(last_kernel, math.sqrt(genes), len(grams)),
        out_shape=[
            jax.ShapeDtypeStruct((owned * side, wide), f32),
            jax.ShapeDtypeStruct((CELL_BLOCKS * side, wide), bf16),
        ],
        in_specs=[ANY] + [VMEM] * (1 + len(grams) + len(zs)),
        out_specs=[VMEM, ANY],
        scratch_shapes=[
            pltpu.VMEM((CELL_BLOCKS, side, 2 * wide), bf16),
            pltpu.VMEM((CELL_BLOCKS * side, wide), bf16),
            pltpu.SemaphoreType.DMA((chunks,)),
            pltpu.SemaphoreType.DMA((chunks,)),
        ],
        compiler_params=pltpu.CompilerParams(vmem_limit_bytes=20 * 2**20),
        name="factors",
    )(split, inverse, *grams, *zs)
    return (cell_factor, gene_factor)


def solution(mesh):
    placed = (
        P(("gx", "gy"), None, None),
        P(("gx", "gy")),
        P(("gx", "gy")),
        P(("gx", "gy")),
        P(),
        P(),
    )
    return jax.shard_map(
        functools.partial(on_device, nx=mesh.shape["gx"], ny=mesh.shape["gy"]),
        mesh=mesh,
        in_specs=placed,
        out_specs=(P(("gx", "gy"), None), P(("gx", "gy"), None)),
        check_vma=False,
    )
```

```python
import functools
import math

import jax
import jax.numpy as jnp
from jax import lax
from jax.experimental import pallas as pl
from jax.experimental.pallas import tpu as pltpu
from jax.sharding import PartitionSpec as P

GROUP = 16
PANEL = 32
EXACT = lax.Precision.HIGHEST
SMEM = pl.BlockSpec(memory_space=pltpu.SMEM)
VMEM = pl.BlockSpec(memory_space=pltpu.VMEM)
ANY = pl.BlockSpec(memory_space=pl.ANY)
ROOMY = pltpu.CompilerParams(vmem_limit_bytes=60 * 2**20)
CELL_BLOCKS = 64


def bit_orders(nx, ny, far_first=False):
    low = (ny - 1).bit_length()
    near, far = list(range(low)), list(range(low, low + (nx - 1).bit_length()))
    swapped = list(near)
    if low >= 3:
        swapped[1], swapped[2] = swapped[2], swapped[1]
    if far_first:
        return [o[:1] + far + o[1:] for o in (near, swapped)]
    return [o + far for o in (near, swapped)]


def place_in(order, owner):
    place = 0
    for bit in order:
        place = place * 2 + ((owner >> bit) & 1)
    return place


def pair_table(owned):
    if owned % 8:
        return [(0, owned // 2, False)]
    return [(0, owned // 4, False), (owned // 2, owned // 8, True), (3 * owned // 4, owned // 8, False)]


def list_tiles(nx, ny, pairs, owned, rows, cols, live, order, slots, list_row, list_tile, list_slot):
    devices = nx * ny
    me = lax.axis_index("gx") * ny + lax.axis_index("gy")

    @pl.loop(0, slots.shape[0] // 16)
    def _(b):
        for j in range(16):
            slots[b * 16 + j] = -1

    total = 0
    for first, each, far_first in pairs:
        size = devices * each // 2
        for part, bits in enumerate(bit_orders(nx, ny, far_first)):
            mine = place_in(bits, me)
            for owner in range(devices):
                place = (place_in(bits, owner) ^ mine) * each
                place += jnp.where(place < size, 0, size) + part * size + total
                for j in range(each):
                    slots[order[owner * owned + first + part * each + j]] = place + j
        total += 4 * size

    room = list_tile.shape[0] // len(pairs)
    ends = [sum(2 * e * devices for _, e, _ in pairs[: k + 1]) for k in range(len(pairs))]

    def step(t, found):
        slot = slots[cols[t]]
        row = rows[t]
        later = []
        for k in range(len(pairs)):
            at = found[k] + k * room
            list_tile[at] = t
            list_row[at] = row
            list_slot[at] = slot
            low = ends[k - 1] if k else 0
            later.append(found[k] + jnp.logical_and(slot >= low, slot < ends[k]).astype(jnp.int32))
        return tuple(later)

    found = lax.fori_loop(0, live, step, (jnp.int32(0),) * len(pairs))
    for k in range(len(pairs)):
        for u in range(GROUP):
            list_tile[found[k] + k * room + u] = 0
            list_row[found[k] + k * room + u] = 0
            list_slot[found[k] + k * room + u] = total
    return found


def add_products(found, first, list_row, list_tile, list_slot, tiles_v, split_v, sums_v):
    @pl.loop(0, (found + GROUP - 1) // GROUP)
    def _(q):
        products = []
        for u in range(GROUP):
            k = first + q * GROUP + u
            product = lax.dot_general(
                tiles_v[list_tile[k]],
                split_v[list_row[k]],
                (((0,), (0,)), ((), ())),
                preferred_element_type=jnp.float32,
            )
            n = product.shape[-1] // 2
            products.append(product[:, :n] + product[:, n:])
        for u in range(GROUP):
            sums_v[list_slot[first + q * GROUP + u]] += products[u]


def zero(ref):
    many = max(d for d in range(1, 9) if ref.shape[0] % d == 0)

    @pl.loop(0, ref.shape[0] // many)
    def _(b):
        for j in range(many):
            ref[b * many + j] = jnp.zeros(ref.shape[1:], ref.dtype)


def add_and_save(pairs, found, list_row, list_tile, list_slot, tiles_v, split_v, sums_v, pieces, sem):
    saves = []
    base = 0
    room = list_tile.shape[0] // len(pairs)
    for p in range(len(pairs)):
        add_products(found[p], p * room, list_row, list_tile, list_slot, tiles_v, split_v, sums_v)
        size = pieces[8 * p].shape[0]
        for k in (5, 7, 4, 6, 1, 3, 0, 2):
            at = pl.ds(base + k * size, size)
            to = pieces[8 * p + k].at[pl.ds(0, size)]
            saves.append(pltpu.make_async_copy(sums_v.at[at], to, sem.at[8 * p + k]))
            saves[-1].start()
        base += 8 * size
    for s in saves:
        s.wait()


def first_kernel(nx, ny, pairs, owned, rows, cols, count, order, tiles, sketch, *refs):
    n_pieces = 8 * len(pairs)
    pieces, split_out = refs[:n_pieces], refs[n_pieces]
    (
        sketch_v, tiles_v, y_v, split_v, sums_v, gram_v, slots, list_row, list_tile, list_slot,
        sem_s, sem_t, sem_y, sem_p, sem_g,
    ) = refs[n_pieces + 1 :]
    cell_blocks = split_v.shape[0]
    live = count[0]
    groups = (live + GROUP - 1) // GROUP

    def load_tiles(g):
        at = pl.ds(g * GROUP, GROUP)
        return pltpu.make_async_copy(tiles.at[at], tiles_v.at[at], sem_t.at[g])

    @pl.loop(0, groups)
    def _(g):
        load_tiles(g).start()
        for u in range(GROUP):
            t = g * GROUP + u
            pltpu.make_async_copy(sketch.at[cols[t]], sketch_v.at[t], sem_s.at[g]).start()

    zero(y_v)
    found = list_tiles(nx, ny, pairs, owned, rows, cols, live, order, slots, list_row, list_tile, list_slot)

    @pl.loop(0, groups)
    def _(g):
        load_tiles(g).wait()
        at = pl.ds(g * GROUP, GROUP)
        pltpu.make_async_copy(sketch.at[pl.ds(0, GROUP)], sketch_v.at[at], sem_s.at[g]).wait()
        products = []
        for u in range(GROUP):
            t = g * GROUP + u
            products.append(jnp.dot(tiles_v[t], sketch_v[t], preferred_element_type=jnp.float32))
        for u in range(GROUP):
            t = g * GROUP + u
            y_v[jnp.where(t < live, rows[t], cell_blocks)] += products[u]

    gram_v[...] = jnp.zeros_like(gram_v)

    turns = cell_blocks // 8
    share = sums_v.shape[0] // turns

    @pl.loop(0, turns)
    def _(b):
        for j in range(share):
            sums_v[b * share + j] = jnp.zeros(sums_v.shape[1:], sums_v.dtype)
        at = pl.ds(b * 8, 8)
        y = y_v[at]
        high = y.astype(jnp.bfloat16)
        low = (y - high.astype(jnp.float32)).astype(jnp.bfloat16)
        both = jnp.concatenate([high, low], axis=-1)
        split_v[at] = both
        rows = y.shape[0] * y.shape[1]
        gram_v[0] += lax.dot_general(
            high.reshape(rows, -1), both.reshape(rows, -1), (((0,), (0,)), ((), ())), preferred_element_type=jnp.float32
        )

    save_split = pltpu.make_async_copy(split_v, split_out, sem_y)
    save_split.start()
    n = y_v.shape[-1]
    cross = gram_v[0, :, n:]
    gram_v[0, :, :n] += cross + cross.T
    rider = pieces[-3]
    save_gram = pltpu.make_async_copy(gram_v.at[:, :, pl.ds(0, n)], rider.at[pl.ds(rider.shape[0] - 1, 1)], sem_g)
    save_gram.start()
    add_and_save(pairs, found, list_row, list_tile, list_slot, tiles_v, split_v, sums_v, pieces, sem_p)
    save_split.wait()
    save_gram.wait()


def second_kernel(nx, ny, pairs, owned, rows, cols, count, order, tiles, split, *refs):
    pieces = refs[: 8 * len(pairs)]
    tiles_v, split_v, sums_v, slots, list_row, list_tile, list_slot, sem_t, sem_y, sem_p = refs[8 * len(pairs) :]
    live = count[0]
    load_split = pltpu.make_async_copy(split, split_v, sem_y)
    load_tiles = pltpu.make_async_copy(tiles, tiles_v, sem_t)
    load_split.start()
    load_tiles.start()
    zero(sums_v)
    found = list_tiles(nx, ny, pairs, owned, rows, cols, live, order, slots, list_row, list_tile, list_slot)
    load_split.wait()
    load_tiles.wait()
    add_and_save(pairs, found, list_row, list_tile, list_slot, tiles_v, split_v, sums_v, pieces, sem_p)


def combine_kernel(counts, *refs):
    out = refs[-1]
    first = row = 0
    for terms, size in counts:
        total = refs[first][...]
        for k in range(1, terms):
            total += refs[first + k][...]
        out[pl.ds(row, size)] = total
        first += terms
        row += size


def inverse_factor(gram, beside=lambda panel: None):
    n = gram.shape[0]
    row = lax.broadcasted_iota(jnp.int32, (PANEL, n), 0)
    eye = lax.broadcasted_iota(jnp.int32, (n, n), 0) == lax.broadcasted_iota(jnp.int32, (n, n), 1)
    rest = jnp.concatenate([gram, eye.astype(jnp.float32)], axis=1)
    done = []
    for p in range(0, n, PANEL):
        a, w = rest[:PANEL, :n], rest[:PANEL, n:]
        columns = [jnp.broadcast_to(a[:, p + t : p + t + 1], (PANEL, n)) for t in range(PANEL)]
        scale = jnp.zeros((PANEL, n), jnp.float32)
        for s in range(PANEL):
            pivot = columns[s][s : s + 1]
            scale = jnp.where(row == s, lax.rsqrt(pivot), scale)
            if s + 1 < PANEL:
                factor = jnp.where(row > s, columns[s] * (1.0 / pivot), 0.0)
                for t in range(s + 1, PANEL):
                    columns[t] = columns[t] - factor * columns[t][s : s + 1]
                a = a - factor * a[s : s + 1]
                w = w - factor * w[s : s + 1]
        a, w = a * scale, w * scale
        done.append(w)
        beside(p // PANEL)
        if p + PANEL < n:
            update = lax.dot_general(
                a, jnp.concatenate([a, w], axis=1), (((0,), (0,)), ((), ())),
                precision=EXACT, preferred_element_type=jnp.float32,
            )
            rest = rest[PANEL:] - update[p + PANEL :]
    return jnp.concatenate(done, axis=0)


def times_transposed(x, w):
    return lax.dot_general(x, w, (((1,), (1,)), ((), ())), precision=EXACT, preferred_element_type=jnp.float32)


def total_of(refs):
    return functools.reduce(jnp.add, [r[...].reshape(r.shape[-2:]) for r in refs])


def factor_kernel(scale, *refs):
    gram, out = refs[:-1], refs[-1]
    out[...] = (inverse_factor(total_of(gram)) * scale).T


def owned_kernel(counts, has_gram, inverse, *refs):
    gram, terms, (z_out, gram_out) = refs[:has_gram], refs[has_gram:-2], refs[-2:]
    rows = []
    first = 0
    for k in counts:
        rows.append(functools.reduce(jnp.add, [t[...] for t in terms[first : first + k]]))
        first += k
    raw = jnp.concatenate(rows, axis=0) if len(rows) > 1 else rows[0]
    raw = raw.reshape(-1, raw.shape[-1])
    z = jnp.dot(raw, inverse[...], precision=EXACT, preferred_element_type=jnp.float32)
    z_out[...] = z
    g = lax.dot_general(z, z, (((0,), (0,)), ((), ())), precision=EXACT, preferred_element_type=jnp.float32)
    if has_gram:
        g += gram[0][0]
    gram_out[0] = g


def last_kernel(scale, n_grams, split, inverse, *refs):
    split_v, out_v, sem_in, sem_out = refs[-4:]
    grams, zs = refs[:n_grams], refs[n_grams:-6]
    out, cells = refs[-6:-4]
    chunks = sem_in.shape[0]
    blocks, side, both = split_v.shape
    chunk, n = blocks // chunks, both // 2
    rows = chunk * side
    loads, saves = [], []
    for c in range(chunks):
        at = pl.ds(c * chunk, chunk)
        loads.append(pltpu.make_async_copy(split.at[at], split_v.at[at], sem_in.at[c]))
        at = pl.ds(c * rows, rows)
        saves.append(pltpu.make_async_copy(out_v.at[at], cells.at[at], sem_out.at[c]))
        loads[c].start()
    high = inverse[...].astype(jnp.bfloat16)
    low = (inverse[...] - high.astype(jnp.float32)).astype(jnp.bfloat16)
    right = jnp.concatenate(
        [jnp.concatenate([high, low], axis=1), jnp.concatenate([high, jnp.zeros_like(low)], axis=1)], axis=0
    )

    def cell_rows(c):
        loads[c].wait()
        y = split_v[pl.ds(c * chunk, chunk)].reshape(rows, both)
        g = jnp.dot(y, right, preferred_element_type=jnp.float32)
        out_v[pl.ds(c * rows, rows), :] = (g[:, :n] + g[:, n:]).astype(out_v.dtype)
        saves[c].start()

    w = inverse_factor(total_of(grams), cell_rows) * scale
    at = 0
    for z in zs:
        out[pl.ds(at, z.shape[0]), :] = times_transposed(z[...], w)
        at += z.shape[0]
    for save in saves:
        save.wait()


def cost(microseconds):
    return pl.CostEstimate(flops=int(microseconds * 1e9), bytes_accessed=int(microseconds * 3e6), transcendentals=0)


def on_device(tiles, tile_rows, tile_cols, tile_counts, block_order, sketch, nx, ny):
    slots_all, side, _ = tiles.shape
    genes, wide = sketch.shape
    blocks = genes // side
    devices = nx * ny
    owned = blocks // devices
    table = pair_table(owned)
    orders = bit_orders(nx, ny)
    early_pairs, late_pairs = table[:2], table[2:]
    f32, bf16 = jnp.float32, jnp.bfloat16

    def piece_shapes(pairs, rider):
        sizes = [devices * each // 4 for _, each, _ in pairs for _ in range(8)]
        sizes[-3] += rider
        return [jax.ShapeDtypeStruct((n, side, wide), f32) for n in sizes]

    def list_scratch(pairs):
        room = slots_all + GROUP
        return [pltpu.SMEM((blocks,), jnp.int32)] + [pltpu.SMEM((len(pairs) * room,), jnp.int32)] * 3

    def sums_scratch(pairs):
        return pltpu.VMEM((sum(2 * each for _, each, _ in pairs) * devices + 8, side, wide), f32)

    def swap(value, bit):
        partner = 1 << bit
        if partner < ny:
            return lax.ppermute(value, "gy", [(i, i ^ partner) for i in range(ny)])
        partner //= ny
        return lax.ppermute(value, "gx", [(i, i ^ partner) for i in range(nx)])

    *early, split = pl.pallas_call(
        functools.partial(first_kernel, nx, ny, early_pairs, owned),
        out_shape=piece_shapes(early_pairs, 1)
        + [jax.ShapeDtypeStruct((CELL_BLOCKS, side, 2 * wide), bf16)],
        in_specs=[SMEM] * 4 + [ANY] * 2,
        out_specs=[ANY] * (8 * len(early_pairs) + 1),
        scratch_shapes=[
            pltpu.VMEM((slots_all, side, wide), bf16),
            pltpu.VMEM((slots_all, side, side), bf16),
            pltpu.VMEM((CELL_BLOCKS + 1, side, wide), f32),
            pltpu.VMEM((CELL_BLOCKS, side, 2 * wide), bf16),
            sums_scratch(early_pairs),
            pltpu.VMEM((1, wide, 2 * wide), f32),
            *list_scratch(early_pairs),
            pltpu.SemaphoreType.DMA((slots_all // GROUP,)),
            pltpu.SemaphoreType.DMA((slots_all // GROUP,)),
            pltpu.SemaphoreType.DMA,
            pltpu.SemaphoreType.DMA((8 * len(early_pairs),)),
            pltpu.SemaphoreType.DMA,
        ],
        compiler_params=ROOMY,
        cost_estimate=cost(4.0),
        name="tile_products",
    )(tile_rows, tile_cols, tile_counts, block_order, tiles, sketch.reshape(blocks, side, wide))

    done_before = [tile_counts]

    def follows(value):
        return lax.optimization_barrier((value, done_before[0]))[0]

    def note(value):
        done_before[0] = value
        return value

    bits = orders[0]
    shared = next(k for k in range(1, len(bits)) if all(o[k:] == bits[k:] for o in orders))
    orders_of = [bit_orders(nx, ny, far_first) for _, _, far_first in table]
    state = {}

    def begin(pair, *arrays):
        kept, quarters = arrays[:4], arrays[4:]
        half = kept[0].shape[0]
        terms = [[[(kept[2 * part + upper], 0)] for upper in range(2)] for part in range(2)]
        state[pair] = [1, half, terms, []]
        if quarters[1].shape[0] > half:
            state[pair][3] = [(quarters[1], half)]

        for k in (1, 3, 0, 2):
            got = swap(quarters[k], orders_of[pair][0][0])
            terms[k // 2][k % 2].append((got, 0))
            if k == 1 and state[pair][3]:
                state[pair][3].append((got, half))

    def wait(pairs):
        found = []
        for pair in pairs:
            _, _, terms, rider = state[pair]
            for array, _ in [terms[part][1][-1] for part in range(2)] + rider[-1:]:
                if not any(array is f for f in found):
                    found.append(array)
        ready = lax.optimization_barrier((*found, done_before[0]))

        def swapped(term):
            return next(((r, term[1]) for f, r in zip(found, ready) if f is term[0]), term)

        for pair in pairs:
            step, size, terms, rider = state[pair]
            terms = [[[swapped(t) for t in upper] for upper in part] for part in terms]
            state[pair] = [step, size, terms, [swapped(t) for t in rider]]

    def combine(groups):
        counts = tuple((len(terms), size) for terms, size in groups)
        specs, arrays = [], []
        for terms, size in groups:
            for array, at in terms:
                specs.append(pl.BlockSpec((size, side, wide), functools.partial(lambda place, _: (place, 0, 0), at // size)))
                arrays.append(array)
        rows = sum(size for _, size in groups)
        return pl.pallas_call(
            functools.partial(combine_kernel, counts),
            grid=(1,),
            out_shape=jax.ShapeDtypeStruct((rows, side, wide), f32),
            in_specs=specs,
            out_specs=pl.BlockSpec((rows, side, wide), lambda _: (0, 0, 0)),
            compiler_params=pltpu.CompilerParams(vmem_limit_bytes=24 * 2**20),
            cost_estimate=cost(0.01),
            name="combine",
        )(*arrays)

    def halves(size, base, got):
        cut = size // 2
        return [[(array, at + upper * cut) for array, at in (base, got)] for upper in range(2)]

    def send_apart(pair, carrier=0):
        step, size, terms, rider = state[pair]
        sent, got = [], []
        for part in range(2):
            groups = [(terms[part][1], size)] + ([(rider, 1)] if rider and part == carrier else [])
            sent.append(note(combine(groups)))
            got.append(swap(sent[part], orders_of[pair][part][step]))
        base = [combine([(terms[part][0], size)]) for part in range(2)]
        rider = [(sent[carrier], size), (got[carrier], size)] if rider else []
        state[pair] = [step + 1, size // 2, [halves(size, (base[part], 0), (got[part], 0)) for part in range(2)], rider]

    def hand_over(pair, other):
        state[other][3], state[pair][3] = state[pair][3], []

    def send_both_upper(pair):
        step, size, terms, rider = state[pair]
        sent = note(combine([(terms[part][1], size) for part in range(2)] + ([(rider, 1)] if rider else [])))
        return sent, swap(sent, orders_of[pair][0][step])

    def keep_both_lower(pair, sent, got):
        step, size, terms, rider = state[pair]
        base = combine([(terms[part][0], size) for part in range(2)])
        rider = [(sent, 2 * size), (got, 2 * size)] if rider else []
        state[pair] = [step + 1, size // 2, [halves(size, (base, part * size), (got, part * size)) for part in range(2)], rider]

    def send_both(pair):
        keep_both_lower(pair, *send_both_upper(pair))

    def term_specs(groups):
        specs, arrays = [], []
        for terms, size in groups:
            for array, at in terms:
                specs.append(pl.BlockSpec((size, side, wide), functools.partial(lambda place, _: (place, 0, 0), at // size)))
                arrays.append(array)
        return specs, arrays

    def owners(pairs, inverse, gram=()):
        groups = [(state[p][2][part][0], max(1, 2 * state[p][1])) for p in pairs for part in range(2)]
        specs, arrays = term_specs(groups)
        rows = sum(size for _, size in groups) * side
        whole = pl.BlockSpec((wide, wide), lambda _: (0, 0))
        square = pl.BlockSpec((1, wide, wide), lambda _: (0, 0, 0))
        z, gram = pl.pallas_call(
            functools.partial(owned_kernel, [len(terms) for terms, _ in groups], len(gram)),
            grid=(1,),
            out_shape=[jax.ShapeDtypeStruct((rows, wide), f32), jax.ShapeDtypeStruct((1, wide, wide), f32)],
            in_specs=[whole] + [square] * len(gram) + specs,
            out_specs=[pl.BlockSpec((rows, wide), lambda _: (0, 0)), square],
            compiler_params=pltpu.CompilerParams(vmem_limit_bytes=24 * 2**20),
            cost_estimate=cost(0.5),
            name="owned_gram",
        )(inverse, *gram, *arrays)
        return z, note(gram)

    cells_all = CELL_BLOCKS * side * devices

    def late_products(pairs):
        return pl.pallas_call(
            functools.partial(second_kernel, nx, ny, pairs, owned),
            out_shape=piece_shapes(pairs, 0),
            in_specs=[SMEM] * 4 + [ANY] * 2,
            out_specs=[ANY] * (8 * len(pairs)),
            scratch_shapes=[
                pltpu.VMEM((slots_all, side, side), bf16),
                pltpu.VMEM((CELL_BLOCKS, side, 2 * wide), bf16),
                sums_scratch(pairs),
                *list_scratch(pairs),
                pltpu.SemaphoreType.DMA,
                pltpu.SemaphoreType.DMA,
                pltpu.SemaphoreType.DMA((8 * len(pairs),)),
            ],
            compiler_params=pltpu.CompilerParams(vmem_limit_bytes=36 * 2**20),
            cost_estimate=cost(4.0),
            name="late_products",
        )(tile_rows, tile_cols, tile_counts, block_order, tiles, follows(split))

    def cell_inverse(pair):
        specs, arrays = term_specs([(state[pair][3], 1)])
        return note(
            pl.pallas_call(
                functools.partial(factor_kernel, math.sqrt(cells_all)),
                grid=(1,),
                out_shape=jax.ShapeDtypeStruct((wide, wide), f32),
                in_specs=specs,
                out_specs=pl.BlockSpec((wide, wide), lambda _: (0, 0)),
                cost_estimate=cost(1.5),
                name="cell_cholesky",
            )(follows(arrays[0]), *arrays[1:])
        )

    begin(0, *early[:8])
    if len(table) == 1:
        for step in range(1, len(bits)):
            wait([0])
            send_apart(0) if step < shared else send_both(0)
        wait([0])
        inverse = cell_inverse(0)
        zs, gene_gram = [None], None
        zs[0], gene_gram = owners([0], inverse)
    else:
        begin(1, *early[8:])
        wait([0])
        send_apart(0)
        wait([1])
        send_both(1)
        late = late_products(late_pairs)
        note(late[0])
        begin(2, *late)
        wait([0])
        send_apart(0)
        wait([1])
        send_both(1)
        wait([2])
        send_apart(2)
        wait([0, 1, 2])
        hand_over(1, 2)
        send_both(0)
        send_apart(2)
        send_apart(1)
        wait([0, 1, 2])
        hand_over(2, 1)
        send_both(0)
        send_both(2)
        send_apart(1, 1)
        wait([0, 1, 2])
        send_both(2)
        inverse = cell_inverse(1)
        z_early, gene_gram = owners([0, 1], inverse)
        wait([2])
        z_late, gene_gram = owners([2], inverse, (gene_gram,))
        zs = [z_early, z_late]

    grams = [gene_gram]
    for k, bit in enumerate(bits):
        if k:
            grams = [combine([([(g, 0) for g in grams], 1)])]
        grams.append(swap(grams[0], bit))
    chunks = wide // PANEL
    gene_factor, cell_factor = pl.pallas_call(
        functools.partial(last_kernel, math.sqrt(genes), len(grams)),
        out_shape=[
            jax.ShapeDtypeStruct((owned * side, wide), f32),
            jax.ShapeDtypeStruct((CELL_BLOCKS * side, wide), bf16),
        ],
        in_specs=[ANY] + [VMEM] * (1 + len(grams) + len(zs)),
        out_specs=[VMEM, ANY],
        scratch_shapes=[
            pltpu.VMEM((CELL_BLOCKS, side, 2 * wide), bf16),
            pltpu.VMEM((CELL_BLOCKS * side, wide), bf16),
            pltpu.SemaphoreType.DMA((chunks,)),
            pltpu.SemaphoreType.DMA((chunks,)),
        ],
        compiler_params=pltpu.CompilerParams(vmem_limit_bytes=20 * 2**20),
        name="factors",
    )(split, inverse, *grams, *zs)
    return (cell_factor, gene_factor)


def solution(mesh):
    placed = (
        P(("gx", "gy"), None, None),
        P(("gx", "gy")),
        P(("gx", "gy")),
        P(("gx", "gy")),
        P(),
        P(),
    )
    return jax.shard_map(
        functools.partial(on_device, nx=mesh.shape["gx"], ny=mesh.shape["gy"]),
        mesh=mesh,
        in_specs=placed,
        out_specs=(P(("gx", "gy"), None), P(("gx", "gy"), None)),
        check_vma=False,
    )
```
